128 devices in a mesh: lon: 16 (over x, z_lo, core), lat: 8 (over y, z_hi).
Axes of the slice: x: 4, y: 4, z: 4 (z_hi: 2, z_lo: 2; z = z_hi * 2 + z_lo), core: 2. Of those that a mesh axis runs over, the one named last changes fastest.
Arguments:
- tracers: bfloat16 [2, 4, 1024, 16384], P(None, None, 'lat', 'lon'), may hold values from -6 to 6
- interp: bfloat16 [1024, 256, 128], P('lat'), may hold values from -0.375 to 0.375
- lat_weight: float32 [1024, 128], P('lat', 'lon'), may hold values from 0 to 1
- lat_row: int32 [1024, 128], P('lat', 'lon'), may hold values from 0 to 1022, as said below
- lon_offset: int32 [1024, 128], P('lat', 'lon'), may hold values from -25 to 64, as said below
Outputs:
- advected: bfloat16 [2, 4, 1024, 16384], P(None, None, 'lat', 'lon')
The draws below stay inside these ranges and needn't reach their ends.
Inputs may be any that keep to these rules, and one draw needn't show every extreme that they name: lat_row[j, b] is j - 1 or j, clipped to 0 .. 1022. For rows j < 1024 // 32 (departures across the pole) lon_offset[j, b] lies in 56 .. 64; for other rows, with q = 1 + [j < 128] + 2 * [j < 64], it lies in -(q - 1) * 8 - 1 .. (q - 1) * 8; both ends are taken in every row; over all rows the offsets reach max(64, 24).
All inputs are finite; a program needn't handle non-finite values.
Results may differ from the reference program's by a relative error of at most 0.001.
Values may be sent and summed in bfloat16 or wider, within the bound.
A program may use at most 128 MiB of HBM per device.

```python
import jax
import jax.numpy as jnp

TRACERS = 2
LEVELS = 4
BLK = 128
NLAT = 1024
NLON = 16384
NB = 128
SHARD_BLOCKS = 8


def offset_bounds():
    row_index = jnp.arange(NLAT, dtype=jnp.int32)
    reach_level = 1 + (row_index < NLAT // 8).astype(jnp.int32) + 2 * (row_index < NLAT // 16).astype(jnp.int32)
    extra_blocks = (reach_level - 1) * SHARD_BLOCKS
    crossing = row_index < NLAT // 32
    lowest = jnp.where(crossing, NB // 2 - SHARD_BLOCKS, -extra_blocks - 1)
    highest = jnp.where(crossing, NB // 2, extra_blocks)
    return (lowest, highest)


def draw_lon_offset(key, part):
    key = jax.random.fold_in(key, 11)
    key_value, key_spot = jax.random.split(key)
    lowest, highest = offset_bounds()
    lowest = lowest[:, None]
    highest = highest[:, None]
    raw_bits = jax.random.randint(key_value, (NLAT, NB), 0, 1 << 20)
    offsets = lowest + raw_bits % (highest - lowest + 1)
    marked = jax.random.randint(key_spot, (NLAT, 1), 0, NB)
    column = jnp.arange(NB, dtype=jnp.int32)[None, :]
    offsets = jnp.where(column == marked, lowest, offsets)
    offsets = jnp.where(column == (marked + 1) % NB, highest, offsets)
    return offsets.astype(jnp.int32)


def draw_lat_row(key, part):
    key = jax.random.fold_in(key, 12)
    step_back = jax.random.randint(key, (NLAT, NB), 0, 2)
    row_index = jnp.arange(NLAT, dtype=jnp.int32)[:, None]
    return jnp.clip(row_index - step_back, 0, NLAT - 2).astype(jnp.int32)


def level_of(own_key, extent, cuts, low, largest):
    factor_of = 1.0
    for dim, shards_of in cuts:
        steps = jax.random.uniform(jax.random.fold_in(jax.random.fold_in(own_key, 6), dim), (shards_of,), jnp.float32, low / len(cuts), largest / len(cuts))
        factor_of = factor_of * jnp.repeat(jnp.exp(steps), extent[dim] // shards_of).reshape((-1,) + (1,) * (len(extent) - 1 - dim))
    return factor_of


def normal_values(stream_key, shape, width, reach, cuts=(), kind=jnp.bfloat16):
    level = level_of(stream_key, shape, cuts, -0.22, 0.18) if cuts else 1.0
    entries = jax.random.normal(stream_key, shape, jnp.float32) * width * level
    return jnp.minimum(jnp.maximum(entries, -reach), reach).astype(kind)


def setup_inputs(seed: int = 0) -> dict:
    keys = jax.random.split(jax.random.key(seed), 6)
    return {
        "tracers": normal_values(keys[0], (TRACERS, LEVELS, NLAT, NLON), 1.0, 6.0, ((2, 8), (3, 16))),
        "interp": normal_values(keys[1], (NLAT, 2 * BLK, BLK), (2 * BLK) ** -0.5, 0.375, ((0, 8),)),
        "lat_weight": jnp.clip(1.0 * jax.random.uniform(keys[2], (NLAT, NB), jnp.float32) ** level_of(keys[2], (NLAT, NB), ((0, 8), (1, 16)), -0.2, 0.2), 0.0, 1.0),
        "lat_row": draw_lat_row(jax.random.fold_in(keys[5], 71), 0),
        "lon_offset": draw_lon_offset(jax.random.fold_in(keys[5], 71), 0),
    }


def reference(tracers, interp, lat_weight, lat_row, lon_offset):
    channels = tracers.shape[0] * tracers.shape[1]
    block_count = tracers.shape[3] // BLK
    tiles = tracers.reshape(channels, tracers.shape[2], block_count, BLK).astype(jnp.float32)
    leading = jnp.mod(jnp.arange(block_count, dtype=jnp.int32)[None, :] + lon_offset, block_count).astype(jnp.int32)
    trailing = jnp.mod(leading + 1, block_count).astype(jnp.int32)
    upper_row = (lat_row + 1).astype(jnp.int32)
    lower = jnp.concatenate([tiles[:, lat_row, leading], tiles[:, lat_row, trailing]], axis=-1)
    upper = jnp.concatenate([tiles[:, upper_row, leading], tiles[:, upper_row, trailing]], axis=-1)
    matrices = interp.astype(jnp.float32)
    south_part = jnp.einsum('crbk,rkn->crbn', lower, matrices)
    north_part = jnp.einsum('crbk,rkn->crbn', upper, matrices)
    blend = lat_weight[None, :, :, None]
    result = (1.0 - blend) * south_part + blend * north_part
    return result.reshape(tracers.shape).astype(jnp.bfloat16)
```

```python
import functools

import jax
import jax.numpy as jnp
from jax import lax
from jax.experimental import pallas as pl
from jax.experimental.pallas import tpu as pltpu
from jax.sharding import PartitionSpec as P

BLK = 128
LON = 16
LAT = 8
BLOCKS = 8
CH = 8
ROWS = 128
RIM = ROWS + 2
QROWS = 32
QSRC = QROWS + 2
POLAR = ((56, 17), (-25, 58), (-9, 26), (-9, 26))
POLAR_BASE = (0, 17, 75, 101)
PLAIN = ((-1, 10),) * 4
PLAIN_BASE = (0, 10, 20, 30)
SLOTS = 127
MESH = pl.DeviceIdType.MESH


def pieces(window):
    low, width = window
    out = []
    for dist in range(-4, 10):
        first = max(low, 8 * dist)
        last = min(low + width, 8 * dist + 8)
        if first < last:
            out.append((dist, first - 8 * dist, last - first, first - low))
    return out


def exchange_kernel(tracers, window, x, t32, halo_sem, send_sem, recv_sem, own_sem):
    lon = lax.axis_index("lon")
    lat = lax.axis_index("lat")
    north = lax.rem(lat + LAT - 1, LAT)
    south = lax.rem(lat + 1, LAT)

    def behind(dist):
        return lax.rem(lon - dist + LON, LON)

    barrier = pltpu.get_barrier_semaphore()
    for other in (north, south):
        pl.semaphore_signal(barrier, inc=1, device_id=(lon, other), device_id_type=MESH)
    polar_dists = sorted({s * p[0] % LON for w in POLAR for p in pieces(w) for s in (1, -1) if p[0]})
    plain_dists = sorted({s * p[0] % LON for w in PLAIN for p in pieces(w) for s in (1, -1) if p[0]})

    def greet(dists):
        for d in dists:
            pl.semaphore_signal(barrier, inc=1, device_id=(behind(d), lat), device_id_type=MESH)
        pl.semaphore_wait(barrier, len(dists) + 2)

    @pl.when(lat == 0)
    def _():
        greet(polar_dists)

    @pl.when(lat != 0)
    def _():
        greet(plain_dists)

    for g in range(BLOCKS):
        for rb in range(ROWS // 16):
            for ch in range(CH):
                part = tracers[ch, 16 * rb : 16 * rb + 16, BLK * g : BLK * (g + 1)].astype(jnp.float32)
                t32[g, pl.ds(8 + 128 * rb + ch, 16, stride=8), :] = part

    down = pltpu.make_async_remote_copy(
        src_ref=t32.at[:, pl.ds(8 * ROWS, 8), :], dst_ref=t32.at[:, pl.ds(0, 8), :],
        send_sem=halo_sem.at[0], recv_sem=halo_sem.at[1], device_id=(lon, south), device_id_type=MESH)
    up = pltpu.make_async_remote_copy(
        src_ref=t32.at[:, pl.ds(8, 8), :], dst_ref=t32.at[:, pl.ds(8 * RIM - 8, 8), :],
        send_sem=halo_sem.at[2], recv_sem=halo_sem.at[3], device_id=(lon, north), device_id_type=MESH)
    down.start()
    up.start()
    for g in range(BLOCKS):
        x[g, 16 : 8 * RIM - 16, :] = t32[g, 16 : 8 * RIM - 16, :].astype(jnp.bfloat16)
    down.wait()
    up.wait()
    for g in range(BLOCKS):
        x[g, 0:16, :] = t32[g, 0:16, :].astype(jnp.bfloat16)
        x[g, 8 * RIM - 16 : 8 * RIM, :] = t32[g, 8 * RIM - 16 : 8 * RIM, :].astype(jnp.bfloat16)

    def send(windows, bases):
        copies = []
        count = 0
        for q in range(4):
            for dist, first, blocks, slot in pieces(windows[q]):
                src = x.at[pl.ds(first, blocks), pl.ds(8 * QROWS * q, 8 * QSRC), :]
                dst = window.at[pl.ds(bases[q] + slot, blocks)]
                if dist:
                    copy = pltpu.make_async_remote_copy(
                        src_ref=src, dst_ref=dst, send_sem=send_sem.at[count], recv_sem=recv_sem.at[count],
                        device_id=(behind(dist), lat), device_id_type=MESH)
                    count += 1
                else:
                    copy = pltpu.make_async_copy(src, dst, own_sem.at[q])
                copy.start()
                copies.append(copy)
        for copy in copies:
            copy.wait()

    @pl.when(lat == 0)
    def _():
        send(POLAR, POLAR_BASE)

    @pl.when(lat != 0)
    def _():
        send(PLAIN, PLAIN_BASE)


def interpolate_kernel(lat_row, lon_offset, lat_weight, window, interp, out, held, o32, sems):
    step = pl.program_id(0)
    lat = lax.axis_index("lat")
    quarter = step // 2

    def fetch(q, base, width):
        return pltpu.make_async_copy(window.at[pl.ds(base, width)], held.at[pl.ds(base, width)], sems.at[q])

    for polar, windows, bases in ((True, POLAR, POLAR_BASE), (False, PLAIN, PLAIN_BASE)):
        @pl.when((step == 0) & ((lat == 0) == polar))
        def _(windows=windows, bases=bases):
            for q in range(4):
                fetch(q, bases[q], windows[q][1]).start()

        for q in range(4):
            @pl.when((step == 2 * q) & ((lat == 0) == polar))
            def _(q=q, windows=windows, bases=bases):
                fetch(q, bases[q], windows[q][1]).wait()

    def of_quarter(values):
        return jnp.where(quarter == 0, values[0], jnp.where(quarter == 1, values[1], jnp.where(quarter == 2, values[2], values[3])))

    shift = jnp.where(
        lat == 0,
        of_quarter([b - w[0] for b, w in zip(POLAR_BASE, POLAR)]),
        of_quarter([b - w[0] for b, w in zip(PLAIN_BASE, PLAIN)]),
    )
    first_row = lat * ROWS

    for pair in range(8):
        start = pl.multiple_of(lax.rem(step, 2) * 128 + 16 * pair, 16)
        for half in range(2):
            j = 2 * pair + half
            row = 16 * step + j
            lead, trail = [], []
            for b in range(BLOCKS):
                g = shift + lon_offset[row, b] + b
                lead.append(held[g, pl.ds(start, 32), :])
                trail.append(held[g + 1, pl.ds(start, 32), :])
            lhs = jnp.concatenate([jnp.concatenate(lead, axis=0), jnp.concatenate(trail, axis=0)], axis=1)
            prod = jnp.dot(lhs, interp[j], preferred_element_type=jnp.float32)
            for b in range(BLOCKS):
                w = lat_weight[row, b]
                back = lat_row[row, b] < first_row + row
                c0 = jnp.where(back, 1.0 - w, 0.0)
                c1 = jnp.where(back, w, 1.0 - w)
                c2 = jnp.where(back, 0.0, w)
                at = 32 * b + 8 * half
                o32[b, 8 * j : 8 * j + 8, :] = (
                    c0 * prod[at : at + 8] + c1 * prod[at + 8 : at + 16] + c2 * prod[at + 16 : at + 24]
                )
    for b in range(BLOCKS):
        for ch in range(CH):
            out[ch, :, BLK * b : BLK * (b + 1)] = o32[b, pl.ds(ch, 16, stride=8), :].astype(jnp.bfloat16)


def on_device(tracers, interp, lat_weight, lat_row, lon_offset):
    packed = tracers.reshape(CH, ROWS, BLOCKS * BLK)
    copies = sum(1 for w in POLAR for p in pieces(w) if p[0])
    vmem = pl.BlockSpec(memory_space=pltpu.VMEM)
    smem = pl.BlockSpec(memory_space=pltpu.SMEM)
    anywhere = pl.BlockSpec(memory_space=pl.ANY)
    window = pl.pallas_call(
        exchange_kernel,
        out_shape=jax.ShapeDtypeStruct((SLOTS, 8 * QSRC, BLK), jnp.bfloat16),
        in_specs=[vmem],
        out_specs=anywhere,
        scratch_shapes=[
            pltpu.VMEM((BLOCKS, 8 * RIM, BLK), jnp.bfloat16),
            pltpu.VMEM((BLOCKS, 8 * RIM, BLK), jnp.float32),
            pltpu.SemaphoreType.DMA((4,)),
            pltpu.SemaphoreType.DMA((copies,)),
            pltpu.SemaphoreType.DMA((copies,)),
            pltpu.SemaphoreType.DMA((4,)),
        ],
        compiler_params=pltpu.CompilerParams(collective_id=0, has_side_effects=True, vmem_limit_bytes=40 << 20),
        name="exchange",
    )(packed)
    result = pl.pallas_call(
        interpolate_kernel,
        out_shape=jax.ShapeDtypeStruct((CH, ROWS, BLOCKS * BLK), jnp.bfloat16),
        grid=(8,),
        in_specs=[smem, smem, smem, anywhere, pl.BlockSpec((16, 2 * BLK, BLK), lambda i: (i, 0, 0))],
        out_specs=pl.BlockSpec((CH, 16, BLOCKS * BLK), lambda i: (0, i, 0)),
        scratch_shapes=[
            pltpu.VMEM((SLOTS, 8 * QSRC, BLK), jnp.bfloat16),
            pltpu.VMEM((BLOCKS, 8 * 16, BLK), jnp.float32),
            pltpu.SemaphoreType.DMA((4,)),
        ],
        compiler_params=pltpu.CompilerParams(vmem_limit_bytes=40 << 20),
        name="interpolate",
    )(lat_row, lon_offset, lat_weight, window, interp)
    return result.reshape(tracers.shape)


def solution(mesh):
    return jax.shard_map(
        on_device,
        mesh=mesh,
        in_specs=(
            P(None, None, "lat", "lon"),
            P("lat", None, None),
            P("lat", "lon"),
            P("lat", "lon"),
            P("lat", "lon"),
        ),
        out_specs=P(None, None, "lat", "lon"),
        check_vma=False,
    )
```

```python
import functools

import jax
import jax.numpy as jnp
from jax import lax
from jax.experimental import pallas as pl
from jax.experimental.pallas import tpu as pltpu
from jax.sharding import PartitionSpec as P

BLK = 128
LON = 16
LAT = 8
BLOCKS = 8
CH = 8
ROWS = 128
RIM = ROWS + 2
QROWS = 32
QSRC = QROWS + 2
TILE_ROWS = 8 * QSRC
POLAR_SHIFT = (-56, 25, 9, 9)
POLAR_OWN = (17, 25, 9, 9)
SLOTS = (25, 58, 26, 26)
SIDES = (("n", 2), ("s", 6))
CHUNKS_A = {"n": ((0, 2), (2, 2)), "s": ((4, 2), (6, 2))}
CHUNKS_C = {"n": ((0, 2), (2, 3)), "s": ((5, 2), (7, 2))}
SEMS = 160
RELAY = 40
MESH = pl.DeviceIdType.MESH


def fused_kernel(lat_row, lon_offset, lat_weight, tracers, interp, out,
                 tbuf, mats, t32, w0, w1, w2, w3, relay, o32, load_sem, halo_sem, send_sem, recv_sem):
    lon = lax.axis_index("lon")
    lat = lax.axis_index("lat")
    odd = lax.rem(lon, 2) == 1
    far_z = lax.rem(lax.div(lon, 2), 2) == 1
    inner = odd != far_z
    polar = lat == 0
    relays = (lat == SIDES[0][1]) | (lat == SIDES[1][1])
    wins = (w0, w1, w2, w3)

    def at(lat_index, dist):
        return (lax.rem(lon + dist + LON, LON), lat_index)

    def pick(if_odd, if_even):
        return jnp.where(odd, if_odd, if_even)

    north = lax.rem(lat + LAT - 1, LAT)
    south = lax.rem(lat + 1, LAT)
    sib = at(lat, pick(-1, 1))
    nb = at(lat, pick(1, -1))
    zdist = jnp.where(far_z, -2, 2)
    xdist = jnp.where(far_z, -4, 4)

    load_tracers = pltpu.make_async_copy(tracers, tbuf, load_sem.at[0])
    load_mats = pltpu.make_async_copy(interp, mats, load_sem.at[1])
    load_tracers.start()
    load_mats.start()

    barrier = pltpu.get_barrier_semaphore()

    def greet(devices):
        for d in devices:
            pl.semaphore_signal(barrier, inc=1, device_id=d, device_id_type=MESH)

    greet([(lon, north), (lon, south)])

    @pl.when(polar)
    def _():
        greet([sib, nb, at(lat, zdist), at(lat, 4), at(lat, -4), at(lat, pick(3, -3))] + [(lon, s) for _, s in SIDES])

    @pl.when(jnp.logical_not(polar))
    def _():
        greet([sib, nb])

    @pl.when(relays)
    def _():
        greet([at(0, 0), at(lat, 8), at(lat, pick(-7, 7))])

    load_tracers.wait()
    for g in range(BLOCKS):
        for rb in range(ROWS // 16):
            for ch in range(CH):
                part = tbuf[ch, 16 * rb : 16 * rb + 16, BLK * g : BLK * (g + 1)].astype(jnp.float32)
                t32[g, pl.ds(8 + 128 * rb + ch, 16, stride=8), :] = part

    @pl.when(polar)
    def _():
        pl.semaphore_wait(barrier, 10)

    @pl.when(relays)
    def _():
        pl.semaphore_wait(barrier, 7)

    @pl.when(jnp.logical_not(polar | relays))
    def _():
        pl.semaphore_wait(barrier, 4)

    down = pltpu.make_async_remote_copy(
        src_ref=t32.at[:, pl.ds(8 * ROWS, 8), :], dst_ref=t32.at[:, pl.ds(0, 8), :],
        send_sem=halo_sem.at[0], recv_sem=halo_sem.at[1], device_id=(lon, south), device_id_type=MESH)
    up = pltpu.make_async_remote_copy(
        src_ref=t32.at[:, pl.ds(8, 8), :], dst_ref=t32.at[:, pl.ds(8 * RIM - 8, 8), :],
        send_sem=halo_sem.at[2], recv_sem=halo_sem.at[3], device_id=(lon, north), device_id_type=MESH)
    down.start()
    up.start()

    def pack(q, low, high):
        own = jnp.where(polar, POLAR_OWN[q], 1)
        for g in range(BLOCKS):
            wins[q][own + g, low:high, :] = t32[g, 8 * QROWS * q + low : 8 * QROWS * q + high, :].astype(jnp.bfloat16)

    pack(1, 0, TILE_ROWS)
    pack(2, 0, TILE_ROWS)
    pack(0, 16, TILE_ROWS)
    pack(3, 0, TILE_ROWS - 16)
    down.wait()
    up.wait()
    pack(0, 0, 16)
    pack(3, TILE_ROWS - 16, TILE_ROWS)
    load_mats.wait()

    ids = {}
    sent = []

    def copy(name, src, dst, to):
        index = ids.setdefault(name, len(ids))
        assert index < SEMS, name
        return pltpu.make_async_remote_copy(
            src_ref=src, dst_ref=dst, send_sem=send_sem.at[index], recv_sem=recv_sem.at[index],
            device_id=to, device_id_type=MESH)

    def when(cond, body):
        if cond is None:
            body()
        else:
            pl.when(cond)(body)

    def put(name, src, dst, to, cond=None):
        when(cond, lambda: copy(name, src, dst, to).start())
        sent.append((cond, lambda: copy(name, src, dst, to).wait_send()))

    def got(name, dst, cond=None):
        when(cond, lambda: copy(name, dst, dst, sib).wait_recv())

    def all_sent():
        for cond, wait in sent:
            when(cond, wait)
        sent.clear()

    def span(ref, first, count):
        return ref.at[pl.ds(first, count)]

    def c_wins(q):
        return wins[q], f"c{q}"

    even = jnp.logical_not(odd)
    outer = jnp.logical_not(inner)
    compute = functools.partial(interpolate, lat_row, lon_offset, lat_weight, mats, out, o32, polar, lat * ROWS)

    @pl.when(polar)
    def _():
        put("b sib", span(w1, 25, 8), span(w1, pick(33, 17), 8), sib)
        for q in (2, 3):
            put(f"c{q} sib", span(wins[q], 9, 8), span(wins[q], pick(17, 1), 8), sib)
        for i in range(2):
            put(f"b z{i}", span(w1, 25 + 4 * i, 4), span(w1, jnp.where(far_z, 41, 9) + 4 * i, 4), at(lat, zdist))
        for i in range(2):
            for side, band in SIDES:
                first, count = CHUNKS_A[side][i]
                put(f"a up {side}{i}", span(w0, 17 + first, count), span(relay, 2 * i, count), at(band, 0))
        got("b sib", span(w1, pick(17, 33), 8))
        put("b far", span(w1, pick(24, 25), 9), span(w1, pick(0, 49), 9), at(lat, pick(3, -3)))
        for q in (2, 3):
            got(f"c{q} sib", span(wins[q], pick(1, 17), 8))
            for i in range(2):
                for side, band in SIDES:
                    first, count = CHUNKS_C[side][i]
                    put(f"c{q} up {side}{i}", span(wins[q], pick(8, 9) + first, count),
                        span(relay, 4 + 5 * (q - 2) + 2 * i, count), at(band, 0), inner if q == 2 else None)
        for i in range(2):
            mine = span(w1, jnp.where(far_z, 9, 41) + 4 * i, 4)
            got(f"b z{i}", mine)
            put(f"b x{i}", mine, span(w1, jnp.where(far_z, 41, 9) + 4 * i, 4), at(lat, xdist))
            if i == 0:
                put("c2 nb", span(w2, pick(8, 9), 9), span(w2, pick(0, 17), 9), nb, outer)
        for i in range(2):
            near = jnp.where(far_z, 9, 41) + 4 * i
            to = jnp.where(far_z, pick(17, 1), pick(49, 33)) + 4 * i
            put(f"b fz{i}", span(w1, near, 4), span(w1, to, 4), sib)

        for i in range(2):
            for side, band in SIDES:
                first, count = CHUNKS_A[side][i]
                got(f"a8 down {side}{i}", span(w0, 8 + first, count))
                put(f"a f {side}{i}", span(w0, 8 + first, count), span(w0, first, count), sib, even)
                if side == "n" and i == 0:
                    put("a one", span(w0, 8, 1), span(w0, 16, 1), sib, odd)
        for i in range(2):
            for side, band in SIDES:
                first, count = CHUNKS_A[side][i]
                got(f"a7 down {side}{i}", span(w0, first, count), even)
                got(f"a f {side}{i}", span(w0, first, count), odd)
        got("a9 down", span(w0, 16, 1), odd)
        got("a one", span(w0, 16, 1), even)
        compute(0, w0)

        def finish_c(q):
            for i in range(2):
                for side, band in SIDES:
                    first, count = CHUNKS_C[side][i]
                    got(f"c{q} down {side}{i}", span(wins[q], pick(17, 0) + first, count), inner if q == 2 else None)
            if q == 2:
                got("c2 nb", span(w2, pick(17, 0), 9), outer)
            put(f"c{q} one", span(wins[q], pick(17, 8), 1), span(wins[q], pick(25, 0), 1), sib)
            got(f"c{q} one", span(wins[q], pick(0, 25), 1))

        finish_c(2)
        compute(2, w2)
        for i in range(2):
            far = jnp.where(far_z, 41, 9) + 4 * i
            got(f"b x{i}", span(w1, far, 4))
            to = jnp.where(far_z, pick(49, 33), pick(17, 1)) + 4 * i
            put(f"b fx{i}", span(w1, far, 4), span(w1, to, 4), sib)
        got("b far", span(w1, pick(49, 0), 9))
        put("b one", span(w1, pick(49, 8), 1), span(w1, pick(57, 0), 1), sib)
        finish_c(3)
        compute(3, w3)
        for i in range(2):
            got(f"b fz{i}", span(w1, jnp.where(far_z, pick(1, 17), pick(33, 49)) + 4 * i, 4))
            got(f"b fx{i}", span(w1, jnp.where(far_z, pick(33, 49), pick(1, 17)) + 4 * i, 4))
        got("b one", span(w1, pick(0, 57), 1))
        compute(1, w1)
        all_sent()

    @pl.when(jnp.logical_not(polar))
    def _():
        for q in range(4):
            put(f"left {q}", span(wins[q], 1, 1), span(wins[q], 9, 1), at(lat, -1))
            put(f"right {q}", span(wins[q], 8, 1), span(wins[q], 0, 1), at(lat, 1))

        for side, band in SIDES:
            @pl.when(lat == band)
            def _(side=side, band=band):
                plain = list(sent)
                sent.clear()
                items = [("a", i) for i in range(2)] + [("c2", i) for i in range(2)] + [("c3", i) for i in range(2)]

                def place(kind, i):
                    if kind == "a":
                        return 2 * i, 14 + 2 * i, CHUNKS_A[side][i]
                    base = 4 + 5 * (int(kind[1]) - 2) + 2 * i
                    return base, base + 14, CHUNKS_C[side][i]

                def across(kind, i):
                    slot, over, (first, count) = place(kind, i)
                    cond = inner if kind == "c2" else None
                    got(f"{kind} up {side}{i}", span(relay, slot, count), cond)
                    if kind == "a":
                        put(f"a8 over {side}{i}", span(relay, slot, count), span(relay, over, count), at(lat, 8))
                        put(f"a7 over {side}{i}", span(relay, slot, count), span(relay, over + 14, count), at(lat, -7), odd)
                        if side == "n" and i == 0:
                            put("a9 over", span(relay, slot, 1), span(relay, 32, 1), at(lat, 7), even)
                    else:
                        put(f"{kind} over {side}{i}", span(relay, slot, count), span(relay, over, count), nb, cond)

                def back(kind, i):
                    slot, over, (first, count) = place(kind, i)
                    cond = inner if kind == "c2" else None
                    if kind == "a":
                        got(f"a8 over {side}{i}", span(relay, over, count))
                        put(f"a8 down {side}{i}", span(relay, over, count), span(w0, 8 + first, count), at(0, 0))
                        got(f"a7 over {side}{i}", span(relay, over + 14, count), even)
                        put(f"a7 down {side}{i}", span(relay, over + 14, count), span(w0, first, count), at(0, 0), even)
                        if side == "n" and i == 0:
                            got("a9 over", span(relay, 32, 1), odd)
                            put("a9 down", span(relay, 32, 1), span(w0, 16, 1), at(0, 0), odd)
                    else:
                        q = int(kind[1])
                        got(f"{kind} over {side}{i}", span(relay, over, count), cond)
                        put(f"{kind} down {side}{i}", span(relay, over, count),
                            span(wins[q], pick(17, 0) + first, count), at(0, 0), cond)

                for k in range(len(items) + 1):
                    if k < len(items):
                        across(*items[k])
                    if k >= 1:
                        back(*items[k - 1])
                all_sent()
                sent.extend(plain)

        for q in range(4):
            got(f"left {q}", span(wins[q], 9, 1))
            got(f"right {q}", span(wins[q], 0, 1))
        for q in range(4):
            compute(q, wins[q])
        all_sent()


def interpolate(lat_row, lon_offset, lat_weight, mats, out, o32, polar, first_row, q, window):
    shift = jnp.where(polar, POLAR_SHIFT[q], 1)
    for part in range(2):
        def pair_of_rows(pair, carry, part=part):
            start = pl.multiple_of(128 * part + 16 * pair, 16)
            for half in range(2):
                j = 2 * pair + half
                row = QROWS * q + 16 * part + j
                lead, trail = [], []
                for b in range(BLOCKS):
                    g = shift + lon_offset[b, row] + b
                    if q == 0:
                        g = jnp.maximum(g, 0)
                    lead.append(window[g, pl.ds(start, 32), :])
                    trail.append(window[g + 1, pl.ds(start, 32), :])
                lhs = jnp.concatenate([jnp.concatenate(lead, axis=0), jnp.concatenate(trail, axis=0)], axis=1)
                prod = jnp.dot(lhs, mats[row], preferred_element_type=jnp.float32)
                for b in range(BLOCKS):
                    w = lat_weight[b, row]
                    back = lat_row[b, row] < first_row + row
                    c0 = jnp.where(back, 1.0 - w, 0.0)
                    c1 = jnp.where(back, w, 1.0 - w)
                    c2 = jnp.where(back, 0.0, w)
                    at = 32 * b + 8 * half
                    o32[b, pl.ds(pl.multiple_of(8 * j, 8), 8), :] = (
                        c0 * prod[at : at + 8] + c1 * prod[at + 8 : at + 16] + c2 * prod[at + 16 : at + 24]
                    )
            return carry

        lax.fori_loop(0, 8, pair_of_rows, 0)
        low = QROWS * q + 16 * part
        for b in range(BLOCKS):
            for ch in range(CH):
                out[ch, low : low + 16, BLK * b : BLK * (b + 1)] = o32[b, pl.ds(ch, 16, stride=8), :].astype(jnp.bfloat16)


def on_device(tracers, interp, lat_weight, lat_row, lon_offset):
    packed = tracers.reshape(CH, ROWS, BLOCKS * BLK)
    smem = pl.BlockSpec(memory_space=pltpu.SMEM)
    anywhere = pl.BlockSpec(memory_space=pl.ANY)
    result = pl.pallas_call(
        fused_kernel,
        out_shape=jax.ShapeDtypeStruct((CH, ROWS, BLOCKS * BLK), jnp.bfloat16),
        in_specs=[smem, smem, smem, anywhere, anywhere],
        out_specs=pl.BlockSpec(memory_space=pltpu.VMEM),
        scratch_shapes=[
            pltpu.VMEM((CH, ROWS, BLOCKS * BLK), jnp.bfloat16),
            pltpu.VMEM((ROWS, 2 * BLK, BLK), jnp.bfloat16),
            pltpu.VMEM((BLOCKS, 8 * RIM, BLK), jnp.float32),
        ] + [pltpu.VMEM((n, TILE_ROWS, BLK), jnp.bfloat16) for n in SLOTS] + [
            pltpu.VMEM((RELAY, TILE_ROWS, BLK), jnp.bfloat16),
            pltpu.VMEM((BLOCKS, 8 * 16, BLK), jnp.float32),
            pltpu.SemaphoreType.DMA((2,)),
            pltpu.SemaphoreType.DMA((4,)),
            pltpu.SemaphoreType.DMA((SEMS,)),
            pltpu.SemaphoreType.DMA((SEMS,)),
        ],
        compiler_params=pltpu.CompilerParams(collective_id=0, has_side_effects=True, vmem_limit_bytes=56 << 20),
        name="advect",
    )(lat_row.T, lon_offset.T, lat_weight.T, packed, interp)
    return result.reshape(tracers.shape)


def solution(mesh):
    return jax.shard_map(
        on_device,
        mesh=mesh,
        in_specs=(
            P(None, None, "lat", "lon"),
            P("lat", None, None),
            P("lat", "lon"),
            P("lat", "lon"),
            P("lat", "lon"),
        ),
        out_specs=P(None, None, "lat", "lon"),
        check_vma=False,
    )
```

```python
import functools

import jax
import jax.numpy as jnp
from jax import lax
from jax.experimental import pallas as pl
from jax.experimental.pallas import tpu as pltpu
from jax.sharding import PartitionSpec as P

BLK = 128
LON = 16
LAT = 8
BLOCKS = 8
CH = 8
ROWS = 128
RIM = ROWS + 2
QROWS = 32
QSRC = QROWS + 2
TILE_ROWS = 8 * QSRC
POLAR_SHIFT = (-56, 25, 9, 9)
POLAR_OWN = (17, 25, 9, 9)
SLOTS = (25, 58, 26, 26)
SIDES = (("n", 2, (0, 2)), ("s", 6, (4, 6)))
SEMS = 128
RELAY = 16
MESH = pl.DeviceIdType.MESH


def fused_kernel(lat_row, lon_offset, lat_weight, tracers, interp, out,
                 tbuf, mats, t32, w0, w1, w2, w3, relay, o32, load_sem, halo_sem, send_sem, recv_sem):
    lon = lax.axis_index("lon")
    lat = lax.axis_index("lat")
    odd = lax.rem(lon, 2) == 1
    far_z = lax.rem(lax.div(lon, 2), 2) == 1
    inner = odd != far_z
    polar = lat == 0
    relays = (lat == SIDES[0][1]) | (lat == SIDES[1][1])
    wins = (w0, w1, w2, w3)

    def at(lat_index, dist):
        return (lax.rem(lon + dist + LON, LON), lat_index)

    def pick(if_odd, if_even):
        return jnp.where(odd, if_odd, if_even)

    north = lax.rem(lat + LAT - 1, LAT)
    south = lax.rem(lat + 1, LAT)
    sib = at(lat, pick(-1, 1))
    nb = at(lat, pick(1, -1))
    zdist = jnp.where(far_z, -2, 2)
    xdist = jnp.where(far_z, -4, 4)

    load_tracers = pltpu.make_async_copy(tracers, tbuf, load_sem.at[0])
    load_mats = pltpu.make_async_copy(interp, mats, load_sem.at[1])
    load_tracers.start()
    load_mats.start()

    barrier = pltpu.get_barrier_semaphore()
    even = jnp.logical_not(odd)
    outer = jnp.logical_not(inner)
    one = jnp.int32(1)
    none = jnp.int32(0)

    def greet(*devices):
        for d in devices:
            pl.semaphore_signal(barrier, inc=1, device_id=d, device_id_type=MESH)

    greet((lon, north), (lon, south))

    @pl.when(polar)
    def _():
        greet(sib, at(lat, zdist), at(lat, pick(2, -2)), at(lat, -xdist), at(lat, pick(4, -4)), at(lat, pick(3, -3)))
        pl.when(outer)(lambda: greet(nb))
        pl.when(odd)(lambda: greet(at(lat, 9)))
        for _, band, _ in SIDES:
            greet(at(band, 8), at(band, 0))
            pl.when(even)(lambda band=band: greet(at(band, jnp.where(far_z, 8, 4))))

    @pl.when(jnp.logical_not(polar))
    def _():
        greet(sib, nb)

    @pl.when(relays)
    def _():
        greet(at(0, 0), at(0, pick(1, -1)))
        pl.when(even)(lambda: greet(at(0, jnp.where(far_z, -1, 3))))

    load_tracers.wait()
    for g in range(BLOCKS):
        for rb in range(ROWS // 16):
            for ch in range(CH):
                part = tbuf[ch, 16 * rb : 16 * rb + 16, BLK * g : BLK * (g + 1)].astype(jnp.float32)
                t32[g, pl.ds(8 + 128 * rb + ch, 16, stride=8), :] = part

    def pack(q, low, high):
        own = jnp.where(polar, POLAR_OWN[q], 1)
        for g in range(BLOCKS):
            wins[q][own + g, low:high, :] = t32[g, 8 * QROWS * q + low : 8 * QROWS * q + high, :].astype(jnp.bfloat16)

    pack(1, 0, TILE_ROWS)
    pack(2, 0, TILE_ROWS)

    greeted = 4 + jnp.where(polar, 8 + jnp.where(outer, one, none) + jnp.where(even, one, 2 * one), none)
    greeted = greeted + jnp.where(relays, 2 + jnp.where(even, one, none), none)
    pl.semaphore_wait(barrier, greeted)

    down = pltpu.make_async_remote_copy(
        src_ref=t32.at[:, pl.ds(8 * ROWS, 8), :], dst_ref=t32.at[:, pl.ds(0, 8), :],
        send_sem=halo_sem.at[0], recv_sem=halo_sem.at[1], device_id=(lon, south), device_id_type=MESH)
    up = pltpu.make_async_remote_copy(
        src_ref=t32.at[:, pl.ds(8, 8), :], dst_ref=t32.at[:, pl.ds(8 * RIM - 8, 8), :],
        send_sem=halo_sem.at[2], recv_sem=halo_sem.at[3], device_id=(lon, north), device_id_type=MESH)
    down.start()
    up.start()

    ids = {}
    sent = []

    def copy(name, src, dst, to):
        index = ids.setdefault(name, len(ids))
        assert index < SEMS, name
        return pltpu.make_async_remote_copy(
            src_ref=src, dst_ref=dst, send_sem=send_sem.at[index], recv_sem=recv_sem.at[index],
            device_id=to, device_id_type=MESH)

    def when(cond, body):
        if cond is None:
            body()
        else:
            pl.when(cond)(body)

    def put(name, src, dst, to, cond=None):
        when(cond, lambda: copy(name, src, dst, to).start())
        sent.append((cond, lambda: copy(name, src, dst, to).wait_send()))

    def got(name, dst, cond=None):
        when(cond, lambda: copy(name, dst, dst, sib).wait_recv())

    def all_sent():
        for cond, wait in sent:
            when(cond, wait)
        sent.clear()

    def span(ref, first, count):
        return ref.at[pl.ds(first, count)]

    compute = functools.partial(interpolate, lat_row, lon_offset, lat_weight, mats, out, o32, polar, lat * ROWS)
    pairs = range(0, BLOCKS, 2)

    @pl.when(polar)
    def _():
        def up_c(q, cond=None):
            for i in range(2):
                for side, band, firsts in SIDES:
                    put(f"c{q} up {side}{i}", span(wins[q], 9 + firsts[i], 2), span(relay, 8 + 4 * (q - 2) + 2 * i, 2),
                        at(band, pick(1, -1)), cond)

        for i in pairs:
            put(f"b z{i}", span(w1, 25 + i, 2), span(w1, jnp.where(far_z, 41, 9) + i, 2), at(lat, zdist))
        up_c(2, inner)
        for i in range(0, BLOCKS, 4):
            put(f"b far{i}", span(w1, 25 + i, 4), span(w1, pick(1, 49) + i, 4), at(lat, pick(3, -3)))
        put("b end", span(w1, pick(25, 32), 1), span(w1, pick(57, 0), 1), at(lat, pick(-4, 4)))
        put("b sib", span(w1, 25, 8), span(w1, pick(33, 17), 8), sib)
        put("c2 sib", span(w2, 9, 8), span(w2, pick(17, 1), 8), sib)
        put("c2 end", span(w2, pick(9, 16), 1), span(w2, pick(25, 0), 1), at(lat, pick(-2, 2)))

        for g in range(BLOCKS):
            first = t32[g, 8:16, :]
            w0[17 + g, 0:16, :] = jnp.concatenate([jnp.zeros_like(first), first], axis=0).astype(jnp.bfloat16)
        pack(0, 16, TILE_ROWS)
        for i in range(2):
            for side, band, firsts in SIDES:
                put(f"a8 up {side}{i}", span(w0, 17 + firsts[i], 2), span(relay, 2 * i, 2), at(band, 0))
        for i in range(2):
            for side, band, firsts in SIDES:
                put(f"a7 up {side}{i}", span(w0, 17 + firsts[i], 2), span(relay, 4 + 2 * i, 2),
                    at(band, jnp.where(far_z, -3, 1)), odd)
        put("a9", span(w0, 17, 1), span(w0, 16, 1), at(lat, -9), even)

        pack(3, 0, TILE_ROWS - 16)
        down.wait()
        up.wait()
        pack(3, TILE_ROWS - 16, TILE_ROWS)
        up_c(3)
        put("c3 sib", span(w3, 9, 8), span(w3, pick(17, 1), 8), sib)
        put("c3 end", span(w3, pick(9, 16), 1), span(w3, pick(25, 0), 1), at(lat, pick(-2, 2)))

        for i in pairs:
            mine = span(w1, jnp.where(far_z, 9, 41) + i, 2)
            got(f"b z{i}", mine)
            put(f"b x{i}", mine, span(w1, jnp.where(far_z, 41, 9) + i, 2), at(lat, xdist))
            put(f"b fz{i}", mine, span(w1, jnp.where(far_z, pick(17, 1), pick(49, 33)) + i, 2), sib)
            if i == 0:
                for k in range(0, BLOCKS, 4):
                    put(f"c2 nb{k}", span(w2, 9 + k, 4), span(w2, pick(1, 17) + k, 4), nb, outer)

        load_mats.wait()

        def finish_c(q, cond=None):
            got(f"c{q} sib", span(wins[q], pick(1, 17), 8))
            got(f"c{q} end", span(wins[q], pick(25, 0), 1))
            for i in range(2):
                for side, _, firsts in SIDES:
                    got(f"c{q} down {side}{i}", span(wins[q], pick(17, 1) + firsts[i], 2), cond)
            if q == 2:
                for k in range(0, BLOCKS, 4):
                    got(f"c2 nb{k}", span(w2, pick(17, 1) + k, 4), outer)
            put(f"c{q} one", span(wins[q], pick(17, 8), 1), span(wins[q], pick(25, 0), 1), sib)
            got(f"c{q} one", span(wins[q], pick(0, 25), 1))

        finish_c(2, inner)
        compute(2, w2)

        for i in range(2):
            for side, _, firsts in SIDES:
                got(f"a8 down {side}{i}", span(w0, 8 + firsts[i], 2))
                put(f"a f {side}{i}", span(w0, 8 + firsts[i], 2), span(w0, firsts[i], 2), sib, even)
                if firsts[i] == 0:
                    put("a one", span(w0, 8, 1), span(w0, 16, 1), sib, odd)
        for i in range(2):
            for side, _, firsts in SIDES:
                got(f"a7 down {side}{i}", span(w0, firsts[i], 2), even)
                got(f"a f {side}{i}", span(w0, firsts[i], 2), odd)
        got("a9", span(w0, 16, 1), odd)
        got("a one", span(w0, 16, 1), even)
        compute(0, w0)

        for i in pairs:
            far = jnp.where(far_z, 41, 9) + i
            got(f"b x{i}", span(w1, far, 2))
            put(f"b fx{i}", span(w1, far, 2), span(w1, jnp.where(far_z, pick(49, 33), pick(17, 1)) + i, 2), sib)
        for i in range(0, BLOCKS, 4):
            got(f"b far{i}", span(w1, pick(49, 1) + i, 4))
        got("b end", span(w1, pick(57, 0), 1))
        put("b one", span(w1, pick(49, 8), 1), span(w1, pick(57, 0), 1), sib)
        finish_c(3)
        compute(3, w3)
        got("b sib", span(w1, pick(17, 33), 8))
        for i in pairs:
            got(f"b fz{i}", span(w1, jnp.where(far_z, pick(1, 17), pick(33, 49)) + i, 2))
            got(f"b fx{i}", span(w1, jnp.where(far_z, pick(33, 49), pick(1, 17)) + i, 2))
        got("b one", span(w1, pick(0, 57), 1))
        compute(1, w1)
        all_sent()

    @pl.when(jnp.logical_not(polar))
    def _():
        def sides(q):
            put(f"left {q}", span(wins[q], 1, 1), span(wins[q], 9, 1), at(lat, -1))
            put(f"right {q}", span(wins[q], 8, 1), span(wins[q], 0, 1), at(lat, 1))

        sides(1)
        sides(2)
        pack(0, 16, TILE_ROWS)
        pack(3, 0, TILE_ROWS - 16)
        down.wait()
        up.wait()
        pack(0, 0, 16)
        pack(3, TILE_ROWS - 16, TILE_ROWS)
        sides(0)
        sides(3)

        for side, band, firsts in SIDES:
            @pl.when(lat == band)
            def _(side=side, firsts=firsts):
                plain = list(sent)
                sent.clear()

                def pass_on(name, i, slot, win, first, dist, cond=None):
                    block = span(relay, slot + 2 * i, 2)
                    got(f"{name} up {side}{i}", block, cond)
                    put(f"{name} down {side}{i}", block, span(win, first + firsts[i], 2), at(0, dist), cond)

                for i in range(2):
                    pass_on("c2", i, 8, w2, pick(17, 1), 0, inner)
                for i in range(2):
                    pass_on("a8", i, 0, w0, 8, -8)
                for i in range(2):
                    pass_on("a7", i, 4, w0, 0, jnp.where(far_z, -8, -4), even)
                for i in range(2):
                    pass_on("c3", i, 12, w3, pick(17, 1), 0)
                all_sent()
                sent.extend(plain)

        load_mats.wait()
        for q in (1, 2, 0, 3):
            got(f"left {q}", span(wins[q], 9, 1))
            got(f"right {q}", span(wins[q], 0, 1))
            compute(q, wins[q])
        all_sent()


def interpolate(lat_row, lon_offset, lat_weight, mats, out, o32, polar, first_row, q, window):
    shift = jnp.where(polar, POLAR_SHIFT[q], 1)
    for part in range(2):
        def pair_of_rows(pair, carry, part=part):
            start = pl.multiple_of(128 * part + 16 * pair, 16)
            for half in range(2):
                j = 2 * pair + half
                row = QROWS * q + 16 * part + j
                lead, trail = [], []
                for b in range(BLOCKS):
                    g = shift + lon_offset[b, row] + b
                    if q == 0:
                        g = jnp.maximum(g, 0)
                    lead.append(window[g, pl.ds(start, 32), :])
                    trail.append(window[g + 1, pl.ds(start, 32), :])
                lhs = jnp.concatenate([jnp.concatenate(lead, axis=0), jnp.concatenate(trail, axis=0)], axis=1)
                prod = jnp.dot(lhs, mats[row], preferred_element_type=jnp.float32)
                for b in range(BLOCKS):
                    w = lat_weight[b, row]
                    back = lat_row[b, row] < first_row + row
                    c0 = jnp.where(back, 1.0 - w, 0.0)
                    c1 = jnp.where(back, w, 1.0 - w)
                    c2 = jnp.where(back, 0.0, w)
                    at = 32 * b + 8 * half
                    o32[b, pl.ds(pl.multiple_of(8 * j, 8), 8), :] = (
                        c0 * prod[at : at + 8] + c1 * prod[at + 8 : at + 16] + c2 * prod[at + 16 : at + 24]
                    )
            return carry

        lax.fori_loop(0, 8, pair_of_rows, 0)
        low = QROWS * q + 16 * part
        for b in range(BLOCKS):
            for ch in range(CH):
                out[ch, low : low + 16, BLK * b : BLK * (b + 1)] = o32[b, pl.ds(ch, 16, stride=8), :].astype(jnp.bfloat16)


def on_device(tracers, interp, lat_weight, lat_row, lon_offset):
    packed = tracers.reshape(CH, ROWS, BLOCKS * BLK)
    smem = pl.BlockSpec(memory_space=pltpu.SMEM)
    anywhere = pl.BlockSpec(memory_space=pl.ANY)
    result = pl.pallas_call(
        fused_kernel,
        out_shape=jax.ShapeDtypeStruct((CH, ROWS, BLOCKS * BLK), jnp.bfloat16),
        in_specs=[smem, smem, smem, anywhere, anywhere],
        out_specs=pl.BlockSpec(memory_space=pltpu.VMEM),
        scratch_shapes=[
            pltpu.VMEM((CH, ROWS, BLOCKS * BLK), jnp.bfloat16),
            pltpu.VMEM((ROWS, 2 * BLK, BLK), jnp.bfloat16),
            pltpu.VMEM((BLOCKS, 8 * RIM, BLK), jnp.float32),
        ] + [pltpu.VMEM((n, TILE_ROWS, BLK), jnp.bfloat16) for n in SLOTS] + [
            pltpu.VMEM((RELAY, TILE_ROWS, BLK), jnp.bfloat16),
            pltpu.VMEM((BLOCKS, 8 * 16, BLK), jnp.float32),
            pltpu.SemaphoreType.DMA((2,)),
            pltpu.SemaphoreType.DMA((4,)),
            pltpu.SemaphoreType.DMA((SEMS,)),
            pltpu.SemaphoreType.DMA((SEMS,)),
        ],
        compiler_params=pltpu.CompilerParams(collective_id=0, has_side_effects=True, vmem_limit_bytes=56 << 20),
        name="advect",
    )(lat_row.T, lon_offset.T, lat_weight.T, packed, interp)
    return result.reshape(tracers.shape)


def solution(mesh):
    return jax.shard_map(
        on_device,
        mesh=mesh,
        in_specs=(
            P(None, None, "lat", "lon"),
            P("lat", None, None),
            P("lat", "lon"),
            P("lat", "lon"),
            P("lat", "lon"),
        ),
        out_specs=P(None, None, "lat", "lon"),
        check_vma=False,
    )
```

```python
import functools

import jax
import jax.numpy as jnp
from jax import lax
from jax.experimental import pallas as pl
from jax.experimental.pallas import tpu as pltpu
from jax.sharding import PartitionSpec as P

BLK = 128
LON = 16
LAT = 8
BLOCKS = 8
CH = 8
ROWS = 128
RIM = ROWS + 2
QROWS = 32
QSRC = QROWS + 2
TILE_ROWS = 8 * QSRC
POLAR_SHIFT = (-56, 25, 9, 9)
POLAR_OWN = (17, 25, 9, 9)
SLOTS = (25, 58, 26, 26)
SIDES = (("n", 2, (0, 2)), ("s", 6, (4, 6)))
SEMS = 128
RELAY = 16
MESH = pl.DeviceIdType.MESH


def fused_kernel(lat_row_in, lon_offset_in, lat_weight_in, tracers, interp, out,
                 lat_row, lon_offset, lat_weight, tbuf, mats, t32, w0, w1, w2, w3, relay, o32, load_sem, halo_sem, send_sem, recv_sem):
    lon = lax.axis_index("lon")
    lat = lax.axis_index("lat")
    odd = lax.rem(lon, 2) == 1
    far_z = lax.rem(lax.div(lon, 2), 2) == 1
    inner = odd != far_z
    polar = lat == 0
    relays = (lat == SIDES[0][1]) | (lat == SIDES[1][1])
    wins = (w0, w1, w2, w3)

    def at(lat_index, dist):
        return (lax.rem(lon + dist + LON, LON), lat_index)

    def pick(if_odd, if_even):
        return jnp.where(odd, if_odd, if_even)

    north = lax.rem(lat + LAT - 1, LAT)
    south = lax.rem(lat + 1, LAT)
    sib = at(lat, pick(-1, 1))
    nb = at(lat, pick(1, -1))
    zdist = jnp.where(far_z, -2, 2)
    xdist = jnp.where(far_z, -4, 4)

    load_tracers = pltpu.make_async_copy(tracers, tbuf, load_sem.at[0])
    load_tracers.start()
    loads = [
        pltpu.make_async_copy(src, dst, load_sem.at[1 + i])
        for i, (src, dst) in enumerate(
            ((interp, mats), (lat_row_in, lat_row), (lon_offset_in, lon_offset), (lat_weight_in, lat_weight)))
    ]

    barrier = pltpu.get_barrier_semaphore()
    even = jnp.logical_not(odd)
    outer = jnp.logical_not(inner)
    one = jnp.int32(1)
    none = jnp.int32(0)

    def greet(*devices):
        for d in devices:
            pl.semaphore_signal(barrier, inc=1, device_id=d, device_id_type=MESH)

    greet((lon, north), (lon, south))

    @pl.when(polar)
    def _():
        greet(sib, at(lat, zdist), at(lat, pick(2, -2)), at(lat, -xdist), at(lat, pick(4, -4)), at(1, pick(3, -3) + zdist))
        pl.when(outer)(lambda: greet(nb))
        pl.when(odd)(lambda: greet(at(lat, 9)))
        for _, band, _ in SIDES:
            greet(at(band, 8), at(band, 0))
            pl.when(even)(lambda band=band: greet(at(band, jnp.where(far_z, 8, 4))))

    @pl.when(jnp.logical_not(polar))
    def _():
        greet(sib, nb)

    @pl.when(relays)
    def _():
        greet(at(0, 0), at(0, pick(1, -1)))
        pl.when(even)(lambda: greet(at(0, jnp.where(far_z, -1, 3))))

    @pl.when(lat == 1)
    def _():
        greet(at(0, zdist))

    for load in loads:
        load.start()
    load_tracers.wait()
    for g in range(BLOCKS):
        for rb in range(ROWS // 16):
            for ch in range(CH):
                part = tbuf[ch, 16 * rb : 16 * rb + 16, BLK * g : BLK * (g + 1)].astype(jnp.float32)
                t32[g, pl.ds(8 + 128 * rb + ch, 16, stride=8), :] = part

    def pack(q, low, high):
        own = jnp.where(polar, POLAR_OWN[q], 1)
        for g in range(BLOCKS):
            wins[q][own + g, low:high, :] = t32[g, 8 * QROWS * q + low : 8 * QROWS * q + high, :].astype(jnp.bfloat16)

    pack(1, 0, TILE_ROWS)
    pack(2, 0, TILE_ROWS)

    greeted = 4 + jnp.where(polar, 8 + jnp.where(outer, one, none) + jnp.where(even, one, 2 * one), none)
    greeted = greeted + jnp.where(lat == 1, one, none) + jnp.where(relays, 2 + jnp.where(even, one, none), none)
    pl.semaphore_wait(barrier, greeted)

    down = pltpu.make_async_remote_copy(
        src_ref=t32.at[:, pl.ds(8 * ROWS, 8), :], dst_ref=t32.at[:, pl.ds(0, 8), :],
        send_sem=halo_sem.at[0], recv_sem=halo_sem.at[1], device_id=(lon, south), device_id_type=MESH)
    up = pltpu.make_async_remote_copy(
        src_ref=t32.at[:, pl.ds(8, 8), :], dst_ref=t32.at[:, pl.ds(8 * RIM - 8, 8), :],
        send_sem=halo_sem.at[2], recv_sem=halo_sem.at[3], device_id=(lon, north), device_id_type=MESH)
    down.start()
    up.start()

    ids = {}
    sent = []

    def copy(name, src, dst, to):
        index = ids.setdefault(name, len(ids))
        assert index < SEMS, name
        return pltpu.make_async_remote_copy(
            src_ref=src, dst_ref=dst, send_sem=send_sem.at[index], recv_sem=recv_sem.at[index],
            device_id=to, device_id_type=MESH)

    def when(cond, body):
        if cond is None:
            body()
        else:
            pl.when(cond)(body)

    def span(ref, first, count):
        return ref, first, count

    def block_of(slots):
        ref, first, count = slots
        return ref.at[pl.ds(first, count)]

    def put(name, src, dst, to, cond=None):
        when(cond, lambda: copy(name, block_of(src), block_of(dst), to).start())
        sent.append((name, src[0], src[2], cond))

    def got(name, dst, cond=None):
        when(cond, lambda: copy(name, block_of(dst), block_of(dst), sib).wait_recv())

    def all_sent():
        for name, ref, count, cond in sent:
            block = ref.at[pl.ds(0, count)]
            when(cond, lambda: copy(name, block, block, sib).wait_send())
        sent.clear()

    compute = functools.partial(interpolate, lat_row, lon_offset, lat_weight, mats, out, o32, polar, lat * ROWS)
    pairs = range(0, BLOCKS, 2)

    def finish_c(q, cond=None):
        got(f"c{q} sib", span(wins[q], pick(1, 17), 8))
        got(f"c{q} end", span(wins[q], pick(25, 0), 1))
        for i in range(2):
            for side, _, firsts in SIDES:
                got(f"c{q} down {side}{i}", span(wins[q], pick(17, 1) + firsts[i], 2), cond)
        if q == 2:
            for k in range(0, BLOCKS, 4):
                got(f"c2 nb{k}", span(w2, pick(17, 1) + k, 4), outer)
        put(f"c{q} one", span(wins[q], pick(17, 8), 1), span(wins[q], pick(25, 0), 1), sib)
        got(f"c{q} one", span(wins[q], pick(0, 25), 1))

    @pl.when(polar)
    def _():
        def up_c(q, cond=None):
            for i in range(2):
                for side, band, firsts in SIDES:
                    put(f"c{q} up {side}{i}", span(wins[q], 9 + firsts[i], 2), span(relay, 8 + 4 * (q - 2) + 2 * i, 2),
                        at(band, pick(1, -1)), cond)

        for i in pairs:
            put(f"b z{i}", span(w1, 25 + i, 2), span(w1, jnp.where(far_z, 41, 9) + i, 2), at(lat, zdist))
        up_c(2, inner)
        for i in range(0, BLOCKS, 4):
            put(f"b far{i} out", span(w1, 25 + i, 4), span(relay, i, 4), at(1, zdist))
        put("b end", span(w1, pick(25, 32), 1), span(w1, pick(57, 0), 1), at(lat, pick(-4, 4)))
        put("b sib", span(w1, 25, 8), span(w1, pick(33, 17), 8), sib)
        put("c2 sib", span(w2, 9, 8), span(w2, pick(17, 1), 8), sib)
        put("c2 end", span(w2, pick(9, 16), 1), span(w2, pick(25, 0), 1), at(lat, pick(-2, 2)))

        for g in range(BLOCKS):
            first = t32[g, 8:16, :]
            w0[17 + g, 0:16, :] = jnp.concatenate([jnp.zeros_like(first), first], axis=0).astype(jnp.bfloat16)
        pack(0, 16, TILE_ROWS)
        for i in range(2):
            for side, band, firsts in SIDES:
                put(f"a8 up {side}{i}", span(w0, 17 + firsts[i], 2), span(relay, 2 * i, 2), at(band, 0))
        for i in range(2):
            for side, band, firsts in SIDES:
                put(f"a7 up {side}{i}", span(w0, 17 + firsts[i], 2), span(relay, 4 + 2 * i, 2),
                    at(band, jnp.where(far_z, -3, 1)), odd)
        put("a9", span(w0, 17, 1), span(w0, 16, 1), at(lat, -9), even)

        pack(3, 0, TILE_ROWS - 16)
        down.wait()
        up.wait()
        pack(3, TILE_ROWS - 16, TILE_ROWS)
        up_c(3)
        put("c3 sib", span(w3, 9, 8), span(w3, pick(17, 1), 8), sib)
        put("c3 end", span(w3, pick(9, 16), 1), span(w3, pick(25, 0), 1), at(lat, pick(-2, 2)))

        for i in pairs:
            mine = span(w1, jnp.where(far_z, 9, 41) + i, 2)
            got(f"b z{i}", mine)
            put(f"b x{i}", mine, span(w1, jnp.where(far_z, 41, 9) + i, 2), at(lat, xdist))
            put(f"b fz{i}", mine, span(w1, jnp.where(far_z, pick(17, 1), pick(49, 33)) + i, 2), sib)
            if i == 0:
                for k in range(0, BLOCKS, 4):
                    put(f"c2 nb{k}", span(w2, 9 + k, 4), span(w2, pick(1, 17) + k, 4), nb, outer)
        finish_c(2, inner)

    polar_sent = list(sent)
    sent.clear()

    @pl.when(jnp.logical_not(polar))
    def _():
        def sides(q):
            put(f"left {q}", span(wins[q], 1, 1), span(wins[q], 9, 1), at(lat, -1))
            put(f"right {q}", span(wins[q], 8, 1), span(wins[q], 0, 1), at(lat, 1))

        sides(1)
        sides(2)
        pack(0, 16, TILE_ROWS)
        pack(3, 0, TILE_ROWS - 16)
        down.wait()
        up.wait()
        pack(0, 0, 16)
        pack(3, TILE_ROWS - 16, TILE_ROWS)
        sides(0)
        sides(3)

        @pl.when(lat == 1)
        def _():
            plain = list(sent)
            sent.clear()
            for i in range(0, BLOCKS, 4):
                block = span(relay, i, 4)
                got(f"b far{i} out", block)
                put(f"b far{i}", block, span(w1, pick(1, 49) + i, 4), at(0, zdist + pick(3, -3)))
            all_sent()
            sent.extend(plain)

        for side, band, firsts in SIDES:
            @pl.when(lat == band)
            def _(side=side, firsts=firsts):
                plain = list(sent)
                sent.clear()

                def pass_on(name, i, slot, win, first, dist, cond=None):
                    block = span(relay, slot + 2 * i, 2)
                    got(f"{name} up {side}{i}", block, cond)
                    put(f"{name} down {side}{i}", block, span(win, first + firsts[i], 2), at(0, dist), cond)

                for i in range(2):
                    pass_on("c2", i, 8, w2, pick(17, 1), 0, inner)
                for i in range(2):
                    pass_on("a8", i, 0, w0, 8, -8)
                for i in range(2):
                    pass_on("a7", i, 4, w0, 0, jnp.where(far_z, -8, -4), even)
                for i in range(2):
                    pass_on("c3", i, 12, w3, pick(17, 1), 0)
                all_sent()
                sent.extend(plain)

        for q in range(4):
            got(f"left {q}", span(wins[q], 9, 1))
            got(f"right {q}", span(wins[q], 0, 1))

    plain_sent = list(sent)
    sent.clear()
    sent.extend(polar_sent)

    for load in loads:
        load.wait()
    compute(2, w2)

    @pl.when(polar)
    def _():
        for i in range(2):
            for side, _, firsts in SIDES:
                got(f"a8 down {side}{i}", span(w0, 8 + firsts[i], 2))
                put(f"a f {side}{i}", span(w0, 8 + firsts[i], 2), span(w0, firsts[i], 2), sib, even)
                if firsts[i] == 0:
                    put("a one", span(w0, 8, 1), span(w0, 16, 1), sib, odd)
        for i in range(2):
            for side, _, firsts in SIDES:
                got(f"a7 down {side}{i}", span(w0, firsts[i], 2), even)
                got(f"a f {side}{i}", span(w0, firsts[i], 2), odd)
        got("a9", span(w0, 16, 1), odd)
        got("a one", span(w0, 16, 1), even)

    compute(0, w0)

    @pl.when(polar)
    def _():
        for i in pairs:
            far = jnp.where(far_z, 41, 9) + i
            got(f"b x{i}", span(w1, far, 2))
            put(f"b fx{i}", span(w1, far, 2), span(w1, jnp.where(far_z, pick(49, 33), pick(17, 1)) + i, 2), sib)
        for i in range(0, BLOCKS, 4):
            got(f"b far{i}", span(w1, pick(49, 1) + i, 4))
        got("b end", span(w1, pick(57, 0), 1))
        put("b one", span(w1, pick(49, 8), 1), span(w1, pick(57, 0), 1), sib)
        finish_c(3)

    compute(3, w3)

    @pl.when(polar)
    def _():
        got("b sib", span(w1, pick(17, 33), 8))
        for i in pairs:
            got(f"b fz{i}", span(w1, jnp.where(far_z, pick(1, 17), pick(33, 49)) + i, 2))
            got(f"b fx{i}", span(w1, jnp.where(far_z, pick(33, 49), pick(1, 17)) + i, 2))
        got("b one", span(w1, pick(0, 57), 1))

    compute(1, w1)

    @pl.when(polar)
    def _():
        all_sent()

    sent.extend(plain_sent)

    @pl.when(jnp.logical_not(polar))
    def _():
        all_sent()


def interpolate(lat_row, lon_offset, lat_weight, mats, out, o32, polar, first_row, q, window):
    shift = jnp.where(polar, POLAR_SHIFT[q], 1)
    sublane = lax.broadcasted_iota(jnp.int32, (16, BLK), 0)

    def part_of_rows(part, carry):
        for j in range(16):
            start = pl.multiple_of(128 * part + 16 * (j // 2), 16)
            row = QROWS * q + 16 * part + j
            lead, trail, backs = [], [], []
            for b in range(BLOCKS):
                g = shift + lon_offset[b, row] + b
                if q == 0:
                    g = jnp.maximum(g, 0)
                back = lat_row[b, row] < first_row + row
                backs.append(back)
                if j % 2 == 0:
                    lower = sublane < jnp.where(back, 0, 8)
                else:
                    lower = sublane < jnp.where(back, 8, 16)
                for tiles, slot in ((lead, g), (trail, g + 1)):
                    tiles.append(jnp.where(lower, window[slot, pl.ds(start + 16, 16), :], window[slot, pl.ds(start, 16), :]))
            lhs = jnp.concatenate([jnp.concatenate(lead, axis=0), jnp.concatenate(trail, axis=0)], axis=1)
            prod = jnp.dot(lhs, mats[row], preferred_element_type=jnp.float32)
            for b in range(BLOCKS):
                w = lat_weight[b, row]
                first_south = backs[b] if j % 2 == 0 else jnp.logical_not(backs[b])
                c0 = jnp.where(first_south, 1.0 - w, w)
                c1 = jnp.where(first_south, w, 1.0 - w)
                o32[b, 8 * j : 8 * j + 8, :] = c0 * prod[16 * b : 16 * b + 8] + c1 * prod[16 * b + 8 : 16 * b + 16]
        low = pl.multiple_of(QROWS * q + 16 * part, 16)
        for b in range(BLOCKS):
            for ch in range(CH):
                out[ch, pl.ds(low, 16), BLK * b : BLK * (b + 1)] = o32[b, pl.ds(ch, 16, stride=8), :].astype(jnp.bfloat16)
        return carry

    lax.fori_loop(0, 2, part_of_rows, 0)


def store_kernel(src, dst, sem):
    copy = pltpu.make_async_copy(src, dst, sem)
    copy.start()
    copy.wait()


def on_device(tracers, interp, lat_weight, lat_row, lon_offset):
    packed = tracers.reshape(CH, ROWS, BLOCKS * BLK)
    anywhere = pl.BlockSpec(memory_space=pl.ANY)
    result = pl.pallas_call(
        fused_kernel,
        out_shape=pltpu.VMEM((CH, ROWS, BLOCKS * BLK), jnp.bfloat16),
        in_specs=[anywhere] * 5,
        out_specs=pl.BlockSpec(memory_space=pltpu.VMEM),
        scratch_shapes=[
            pltpu.SMEM((BLOCKS, ROWS), jnp.int32),
            pltpu.SMEM((BLOCKS, ROWS), jnp.int32),
            pltpu.SMEM((BLOCKS, ROWS), jnp.float32),
            pltpu.VMEM((CH, ROWS, BLOCKS * BLK), jnp.bfloat16),
            pltpu.VMEM((ROWS, 2 * BLK, BLK), jnp.bfloat16),
            pltpu.VMEM((BLOCKS, 8 * RIM, BLK), jnp.float32),
        ] + [pltpu.VMEM((n, TILE_ROWS, BLK), jnp.bfloat16) for n in SLOTS] + [
            pltpu.VMEM((RELAY, TILE_ROWS, BLK), jnp.bfloat16),
            pltpu.VMEM((BLOCKS, 8 * 16, BLK), jnp.float32),
            pltpu.SemaphoreType.DMA((5,)),
            pltpu.SemaphoreType.DMA((4,)),
            pltpu.SemaphoreType.DMA((SEMS,)),
            pltpu.SemaphoreType.DMA((SEMS,)),
        ],
        compiler_params=pltpu.CompilerParams(collective_id=0, has_side_effects=True, vmem_limit_bytes=56 << 20),
        name="advect",
    )(lat_row.T, lon_offset.T, lat_weight.T, packed, interp)
    stored = pl.pallas_call(
        store_kernel,
        out_shape=jax.ShapeDtypeStruct((CH, ROWS, BLOCKS * BLK), jnp.bfloat16),
        in_specs=[pl.BlockSpec(memory_space=pltpu.VMEM)],
        out_specs=anywhere,
        scratch_shapes=[pltpu.SemaphoreType.DMA],
        name="store",
    )(result)
    return stored.reshape(tracers.shape)


def solution(mesh):
    return jax.shard_map(
        on_device,
        mesh=mesh,
        in_specs=(
            P(None, None, "lat", "lon"),
            P("lat", None, None),
            P("lat", "lon"),
            P("lat", "lon"),
            P("lat", "lon"),
        ),
        out_specs=P(None, None, "lat", "lon"),
        check_vma=False,
    )
```

```python
import functools

import jax
import jax.numpy as jnp
from jax import lax
from jax.experimental import pallas as pl
from jax.experimental.pallas import tpu as pltpu
from jax.sharding import PartitionSpec as P

BLK = 128
LON = 16
LAT = 8
BLOCKS = 8
CH = 8
ROWS = 128
RIM = ROWS + 2
QROWS = 32
QSRC = QROWS + 2
TILE_ROWS = 8 * QSRC
POLAR_SHIFT = (-56, 25, 9, 9)
POLAR_OWN = (17, 25, 9, 9)
SLOTS = (25, 58, 26, 26)
SIDES = (("n", 2, (0, 2)), ("s", 6, (4, 6)))
PIECES = (("x", 0, 0, 4, 0), ("n", 2, 4, 1, 0), ("s", 6, 5, 1, 0), ("z", 1, 6, 2, 8))
SEMS = 128
RELAY = 16
MESH = pl.DeviceIdType.MESH


def fused_kernel(lat_row_in, lon_offset_in, lat_weight_in, tracers, interp, out,
                 fields, weight, itable, ftable, slot_of, tiles_of, south_of, north_of, tbuf, mats, t32, w0, w1, w2, w3, relay, o32, load_sem, halo_sem, send_sem, recv_sem):
    lon = lax.axis_index("lon")
    lat = lax.axis_index("lat")
    odd = (lon & 1) == 1
    far_z = (lon & 2) == 2
    polar = lat == 0
    relays = (lat == SIDES[0][1]) | (lat == SIDES[1][1])
    wins = (w0, w1, w2, w3)

    def at(lat_index, dist):
        return ((lon + dist) & (LON - 1), lat_index)

    def pick(if_odd, if_even):
        return jnp.where(odd, if_odd, if_even)

    north = (lat - 1) & (LAT - 1)
    south = (lat + 1) & (LAT - 1)
    sib = at(lat, pick(-1, 1))
    nb = at(lat, pick(1, -1))
    zdist = jnp.where(far_z, -2, 2)
    xdist = jnp.where(far_z, -4, 4)

    load_tracers = pltpu.make_async_copy(tracers, tbuf, load_sem.at[0])
    load_tracers.start()
    loads = [
        pltpu.make_async_copy(src, dst, load_sem.at[1 + i])
        for i, (src, dst) in enumerate(
            ((interp, mats), (lat_row_in, fields.at[0]), (lon_offset_in, fields.at[1]), (lat_weight_in, weight)))
    ]

    barrier = pltpu.get_barrier_semaphore()
    even = jnp.logical_not(odd)
    inner = odd != far_z
    outer = jnp.logical_not(inner)
    one = jnp.int32(1)
    none = jnp.int32(0)

    def greet(*devices):
        for d in devices:
            pl.semaphore_signal(barrier, inc=1, device_id=d, device_id_type=MESH)

    top = lat == 0
    bottom = lat == LAT - 1
    pl.when(jnp.logical_not(top))(lambda: greet((lon, north)))
    pl.when(jnp.logical_not(bottom))(lambda: greet((lon, south)))

    @pl.when(polar)
    def _():
        greet(sib, at(lat, zdist), at(lat, pick(2, -2)), at(lat, -xdist), at(lat, pick(4, -4)), at(1, pick(3, -3) + zdist),
              at(1, zdist + 8), at(lat, 8))
        pl.when(outer)(lambda: greet(nb))
        pl.when(odd)(lambda: greet(at(lat, 9)))
        for _, band, _ in SIDES:
            greet(at(band, 8), at(band, 0))
            pl.when(even)(lambda band=band: greet(at(band, jnp.where(far_z, 8, 4))))

    @pl.when(jnp.logical_not(polar))
    def _():
        greet(sib, nb)

    @pl.when(relays)
    def _():
        greet(at(0, 0), at(0, pick(1, -1)))
        pl.when(even)(lambda: greet(at(0, jnp.where(far_z, -1, 3))))

    @pl.when(lat == 1)
    def _():
        greet(at(0, zdist))

    load_tracers.wait()
    for load in loads:
        load.start()
    for g in range(BLOCKS):
        for rb in range(ROWS // 16):
            for ch in range(CH):
                part = tbuf[ch, 16 * rb : 16 * rb + 16, BLK * g : BLK * (g + 1)].astype(jnp.float32)
                t32[g, pl.ds(8 + 128 * rb + ch, 16, stride=8), :] = part

    def pack(q, low, high):
        own = jnp.where(polar, POLAR_OWN[q], 1)
        for g in range(BLOCKS):
            wins[q][own + g, low:high, :] = t32[g, 8 * QROWS * q + low : 8 * QROWS * q + high, :].astype(jnp.bfloat16)

    pack(1, 0, TILE_ROWS)
    pack(2, 0, TILE_ROWS)

    greeted = 4 - jnp.where(top | bottom, one, none) + jnp.where(polar, 9 + jnp.where(outer, one, none) + jnp.where(even, one, 2 * one), none)
    greeted = greeted + jnp.where(lat == 1, 2 * one, none) + jnp.where(relays, 2 + jnp.where(even, one, none), none)
    pl.semaphore_wait(barrier, greeted)

    down = pltpu.make_async_remote_copy(
        src_ref=t32.at[:, pl.ds(8 * ROWS, 8), :], dst_ref=t32.at[:, pl.ds(0, 8), :],
        send_sem=halo_sem.at[0], recv_sem=halo_sem.at[1], device_id=(lon, south), device_id_type=MESH)
    up = pltpu.make_async_remote_copy(
        src_ref=t32.at[:, pl.ds(8, 8), :], dst_ref=t32.at[:, pl.ds(8 * RIM - 8, 8), :],
        send_sem=halo_sem.at[2], recv_sem=halo_sem.at[3], device_id=(lon, north), device_id_type=MESH)
    pl.when(jnp.logical_not(bottom))(lambda: down.start())
    pl.when(jnp.logical_not(top))(lambda: up.start())

    ids = {}
    sent = []

    def copy(name, src, dst, to):
        index = ids.setdefault(name, len(ids))
        assert index < SEMS, name
        return pltpu.make_async_remote_copy(
            src_ref=src, dst_ref=dst, send_sem=send_sem.at[index], recv_sem=recv_sem.at[index],
            device_id=to, device_id_type=MESH)

    def when(cond, body):
        if cond is None:
            body()
        else:
            pl.when(cond)(body)

    def span(ref, first, count):
        return ref, first, count

    def block_of(slots):
        ref, first, count = slots
        return ref.at[pl.ds(first, count)]

    def put(name, src, dst, to, cond=None):
        when(cond, lambda: copy(name, block_of(src), block_of(dst), to).start())
        sent.append((name, src[0], src[2], cond))

    def got(name, dst, cond=None):
        when(cond, lambda: copy(name, block_of(dst), block_of(dst), sib).wait_recv())

    def all_sent_of(entry):
        name, ref, count, cond = entry
        block = ref.at[pl.ds(0, count)]
        when(cond, lambda: copy(name, block, block, sib).wait_send())

    def all_sent():
        for entry in sent:
            all_sent_of(entry)
        sent.clear()

    compute = functools.partial(interpolate, slot_of, tiles_of, south_of, north_of, mats, out, o32)
    pairs = range(0, BLOCKS, 2)

    def tabulate():
        for load in loads:
            load.wait()

        row = lax.broadcasted_iota(jnp.int32, (BLOCKS, ROWS), 1)
        shift = jnp.where(row < QROWS, POLAR_SHIFT[0], jnp.where(row < 2 * QROWS, POLAR_SHIFT[1], POLAR_SHIFT[2]))
        shift = jnp.where(polar, shift, 1)
        back = fields[0] < lat * ROWS + row
        odd_row = (row & 1) == 1
        itable[0] = jnp.maximum(shift + fields[1] + lax.broadcasted_iota(jnp.int32, (BLOCKS, ROWS), 0), 0)
        itable[1] = jnp.where(back, 0, 8) + jnp.where(odd_row, 8, 0)
        first_south = back != odd_row
        ftable[0] = jnp.where(first_south, 1.0 - weight[...], weight[...])
        ftable[1] = jnp.where(first_south, weight[...], 1.0 - weight[...])
        tables = [
            pltpu.make_async_copy(src, dst, load_sem.at[5 + i])
            for i, (src, dst) in enumerate(
                ((itable.at[0], slot_of), (itable.at[1], tiles_of), (ftable.at[0], south_of), (ftable.at[1], north_of)))
        ]
        for table in tables:
            table.start()
        for table in tables:
            table.wait()

    def across_c(q):
        for i in range(2):
            for side, _, firsts in SIDES:
                split = (q, i) == (3, 1)
                got(f"c{q} {side}{i} down", span(wins[q], pick(17, 1) + firsts[i], 2), inner if split else None)
                if split:
                    got(f"c3 nb{side}", span(w3, pick(17, 1) + firsts[i], 2), outer)
        put(f"c{q} one", span(wins[q], pick(17, 8), 1), span(wins[q], pick(25, 0), 1), sib)

    def finish_c(q):
        got(f"c{q} sib", span(wins[q], pick(1, 17), 8))
        got(f"c{q} end", span(wins[q], pick(25, 0), 1))
        got(f"c{q} one", span(wins[q], pick(0, 25), 1))

    def pass_x(i):
        far = jnp.where(far_z, 41, 9) + i
        got(f"b x{i}", span(w1, far, 2))
        put(f"b fx{i}", span(w1, far, 2), span(w1, jnp.where(far_z, pick(49, 33), pick(17, 1)) + i, 2), sib)

    @pl.when(polar)
    def _():
        def up_c(q, i):
            cond = inner if (q, i) == (3, 1) else None
            for side, band, firsts in SIDES:
                put(f"c{q} {side}{i} up", span(wins[q], 9 + firsts[i], 2), span(relay, 8 + 4 * (q - 2) + 2 * i, 2),
                    at(band, pick(1, -1)), cond)
                if cond is not None:
                    put(f"c3 nb{side}", span(w3, 9 + firsts[i], 2), span(w3, pick(1, 17) + firsts[i], 2), nb, outer)

        def up_a7(i):
            for side, band, firsts in SIDES:
                put(f"a7 {side}{i} up", span(w0, 17 + firsts[i], 2), span(relay, 4 + 2 * i, 2),
                    at(band, jnp.where(far_z, -3, 1)), odd)

        def up_a8(ways):
            for way, band, first, count, slot in PIECES:
                if way not in ways:
                    continue
                if way == "x":
                    put(f"a8 {first} down", span(w0, 17 + first, count), span(w0, 8 + first, count), at(band, -8))
                else:
                    put(f"a8 {first} up", span(w0, 17 + first, count), span(relay, slot, count), at(band, zdist if way == "z" else 0))

        def left(*names):
            for name in names:
                for entry in [x for x in sent if x[0] == name]:
                    sent.remove(entry)
                    all_sent_of(entry)

        for i in pairs:
            put(f"b z{i}", span(w1, 25 + i, 2), span(w1, jnp.where(far_z, 41, 9) + i, 2), at(lat, zdist))
        up_c(2, 0)
        up_c(2, 1)
        for i in pairs:
            put(f"b far{i} up", span(w1, pick(31 - i, 25 + i), 2), span(relay, i, 2), at(1, zdist))
        put("b end", span(w1, pick(25, 32), 1), span(w1, pick(57, 0), 1), at(lat, pick(-4, 4)))
        put("b sib", span(w1, 25, 8), span(w1, pick(33, 17), 8), sib)
        put("c2 sib", span(w2, 9, 8), span(w2, pick(17, 1), 8), sib)
        put("c2 end", span(w2, pick(9, 16), 1), span(w2, pick(25, 0), 1), at(lat, pick(-2, 2)))

        for g in range(BLOCKS):
            first = t32[g, 8:16, :]
            w0[17 + g, 0:16, :] = jnp.concatenate([jnp.zeros_like(first), first], axis=0).astype(jnp.bfloat16)
        pack(0, 16, TILE_ROWS)
        up_a8(("x", "z"))
        put("a9", span(w0, 17, 1), span(w0, 16, 1), at(lat, -9), even)

        pack(3, 0, TILE_ROWS - 16)
        down.wait_send()
        up.wait_recv()
        pack(3, TILE_ROWS - 16, TILE_ROWS)
        put("c3 sib", span(w3, 9, 8), span(w3, pick(17, 1), 8), sib)
        put("c3 end", span(w3, pick(9, 16), 1), span(w3, pick(25, 0), 1), at(lat, pick(-2, 2)))

        for i in pairs:
            mine = span(w1, jnp.where(far_z, 9, 41) + i, 2)
            got(f"b z{i}", mine)
            put(f"b x{i}", mine, span(w1, jnp.where(far_z, 41, 9) + i, 2), at(lat, xdist))
            put(f"b fz{i}", mine, span(w1, jnp.where(far_z, pick(17, 1), pick(49, 33)) + i, 2), sib)
            if i == 0:
                left("c2 n0 up", "c2 s0 up")
                up_a8(("n", "s"))
                up_a7(0)
                tabulate()
            if i == 2:
                left("c2 n1 up", "c2 s1 up")
                up_a7(1)
                up_c(3, 0)
            if i == 4:
                left("a7 n1 up", "a7 s1 up")
                up_c(3, 1)
            if i >= 4:
                pass_x(i - 4)
            if i == 4:
                across_c(2)
        finish_c(2)

    polar_sent = list(sent)
    sent.clear()

    @pl.when(jnp.logical_not(polar))
    def _():
        def sides(q):
            put(f"left {q}", span(wins[q], 1, 1), span(wins[q], 9, 1), at(lat, -1))
            put(f"right {q}", span(wins[q], 8, 1), span(wins[q], 0, 1), at(lat, 1))

        passed = []

        def on_the_way(stage):
            plain = list(sent)

            def pass_on(name, slot, count, win, first, dist, cond=None):
                block = span(relay, slot, count)
                got(f"{name} up", block, cond)
                put(f"{name} down", block, span(win, first, count), at(0, dist), cond)

            @pl.when(lat == 1)
            def _():
                sent.clear()
                if stage == 0:
                    pass_on("b far0", 0, 2, w1, pick(7, 49), zdist + pick(3, -3))
                else:
                    for i in pairs[1:]:
                        pass_on(f"b far{i}", i, 2, w1, pick(7 - i, 49 + i), zdist + pick(3, -3))
                    for way, _, first, count, slot in PIECES:
                        if way == "z":
                            pass_on(f"a8 {first}", slot, count, w0, 8 + first, zdist - 8)
                passed.extend((1, x) for x in sent)

            for side, band, firsts in SIDES:
                @pl.when(lat == band)
                def _(side=side, band=band, firsts=firsts):
                    sent.clear()
                    if stage == 0:
                        for i in range(2):
                            pass_on(f"c2 {side}{i}", 8 + 2 * i, 2, w2, pick(17, 1) + firsts[i], 0)
                    else:
                        for way, _, first, count, slot in PIECES:
                            if way == side:
                                pass_on(f"a8 {first}", slot, count, w0, 8 + first, -8)
                        for i in range(2):
                            pass_on(f"a7 {side}{i}", 4 + 2 * i, 2, w0, firsts[i], jnp.where(far_z, -8, -4), even)
                        for i in range(2):
                            pass_on(f"c3 {side}{i}", 12 + 2 * i, 2, w3, pick(17, 1) + firsts[i], 0, inner if i else None)
                    passed.extend((band, x) for x in sent)

            sent.clear()
            sent.extend(plain)

        sides(1)
        sides(2)
        on_the_way(0)
        pack(0, 16, TILE_ROWS)
        pack(3, 0, TILE_ROWS - 16)
        up.wait_send()
        down.wait_recv()

        @pl.when(jnp.logical_not(bottom))
        def _():
            down.wait_send()
            up.wait_recv()

        @pl.when(bottom)
        def _():
            t32[:, 8 * RIM - 8 : 8 * RIM, :] = jnp.zeros((BLOCKS, 8, BLK), jnp.float32)

        pack(0, 0, 16)
        pack(3, TILE_ROWS - 16, TILE_ROWS)
        sides(0)
        sides(3)
        tabulate()
        on_the_way(1)
        plain = list(sent)
        for band in (1, 2, 6):
            @pl.when(lat == band)
            def _(band=band):
                sent.clear()
                sent.extend(x for at_band, x in passed if at_band == band)
                all_sent()

        sent.clear()
        sent.extend(plain)

        for q in range(4):
            got(f"left {q}", span(wins[q], 9, 1))
            got(f"right {q}", span(wins[q], 0, 1))

    plain_sent = list(sent)
    sent.clear()
    sent.extend(polar_sent)

    compute(2, w2)

    @pl.when(polar)
    def _():
        pass_x(4)
        got("b far0 down", span(w1, pick(49, 7), 2))
        put("b one", span(w1, pick(49, 8), 1), span(w1, pick(57, 0), 1), sib)
        for _, _, first, count, _ in PIECES:
            got(f"a8 {first} down", span(w0, 8 + first, count))
            put(f"a f {first}", span(w0, 8 + first, count), span(w0, first, count), sib, even)
            if first == 0:
                put("a one", span(w0, 8, 1), span(w0, 16, 1), sib, odd)
        pass_x(6)
        for i in pairs[1:]:
            got(f"b far{i} down", span(w1, pick(49 + i, 7 - i), 2))
        got("b end", span(w1, pick(57, 0), 1))
        got("b sib", span(w1, pick(17, 33), 8))
        for i in pairs:
            got(f"b fz{i}", span(w1, jnp.where(far_z, pick(1, 17), pick(33, 49)) + i, 2))
            got(f"b fx{i}", span(w1, jnp.where(far_z, pick(33, 49), pick(1, 17)) + i, 2))
        got("b one", span(w1, pick(0, 57), 1))

    compute(1, w1)

    @pl.when(polar)
    def _():
        across_c(3)
        for i in range(2):
            for side, _, firsts in SIDES:
                got(f"a7 {side}{i} down", span(w0, firsts[i], 2), even)
        for _, _, first, count, _ in PIECES:
            got(f"a f {first}", span(w0, first, count), odd)
        got("a9", span(w0, 16, 1), odd)
        got("a one", span(w0, 16, 1), even)

    compute(0, w0)

    @pl.when(polar)
    def _():
        finish_c(3)

    compute(3, w3)

    @pl.when(polar)
    def _():
        all_sent()

    sent.extend(plain_sent)

    @pl.when(jnp.logical_not(polar))
    def _():
        all_sent()


def interpolate(slot_of, tiles_of, south_of, north_of, mats, out, o32, q, window):
    sublane = lax.broadcasted_iota(jnp.int32, (16, BLK), 0)

    def part_of_rows(part, carry):
        for j in range(16):
            start = pl.multiple_of(128 * part + 16 * (j // 2), 16)
            row = QROWS * q + 16 * part + j
            lead, trail = [], []
            for b in range(BLOCKS):
                g = slot_of[b, row]
                lower = sublane < tiles_of[b, row]
                for tiles, slot in ((lead, g), (trail, g + 1)):
                    tiles.append(jnp.where(lower, window[slot, pl.ds(start + 16, 16), :], window[slot, pl.ds(start, 16), :]))
            lhs = jnp.concatenate([jnp.concatenate(lead, axis=0), jnp.concatenate(trail, axis=0)], axis=1)
            prod = jnp.dot(lhs, mats[row], preferred_element_type=jnp.float32)
            for b in range(BLOCKS):
                at = 16 * b
                o32[b, 8 * j : 8 * j + 8, :] = south_of[b, row] * prod[at : at + 8] + north_of[b, row] * prod[at + 8 : at + 16]
        low = pl.multiple_of(QROWS * q + 16 * part, 16)
        for b in range(BLOCKS):
            for ch in range(CH):
                out[ch, pl.ds(low, 16), BLK * b : BLK * (b + 1)] = o32[b, pl.ds(ch, 16, stride=8), :].astype(jnp.bfloat16)
        return carry

    lax.fori_loop(0, 2, part_of_rows, 0)


def on_device(tracers, interp, lat_weight, lat_row, lon_offset):
    packed = tracers.reshape(CH, ROWS, BLOCKS * BLK)
    anywhere = pl.BlockSpec(memory_space=pl.ANY)
    result = pl.pallas_call(
        fused_kernel,
        out_shape=pltpu.VMEM((CH, ROWS, BLOCKS * BLK), jnp.bfloat16),
        in_specs=[anywhere] * 5,
        out_specs=pl.BlockSpec(memory_space=pltpu.VMEM),
        scratch_shapes=[
            pltpu.VMEM((2, BLOCKS, ROWS), jnp.int32),
            pltpu.VMEM((BLOCKS, ROWS), jnp.float32),
            pltpu.VMEM((2, BLOCKS, ROWS), jnp.int32),
            pltpu.VMEM((2, BLOCKS, ROWS), jnp.float32),
            pltpu.SMEM((BLOCKS, ROWS), jnp.int32),
            pltpu.SMEM((BLOCKS, ROWS), jnp.int32),
            pltpu.SMEM((BLOCKS, ROWS), jnp.float32),
            pltpu.SMEM((BLOCKS, ROWS), jnp.float32),
            pltpu.VMEM((CH, ROWS, BLOCKS * BLK), jnp.bfloat16),
            pltpu.VMEM((ROWS, 2 * BLK, BLK), jnp.bfloat16),
            pltpu.VMEM((BLOCKS, 8 * RIM, BLK), jnp.float32),
        ] + [pltpu.VMEM((n, TILE_ROWS, BLK), jnp.bfloat16) for n in SLOTS] + [
            pltpu.VMEM((RELAY, TILE_ROWS, BLK), jnp.bfloat16),
            pltpu.VMEM((BLOCKS, 8 * 16, BLK), jnp.float32),
            pltpu.SemaphoreType.DMA((9,)),
            pltpu.SemaphoreType.DMA((4,)),
            pltpu.SemaphoreType.DMA((SEMS,)),
            pltpu.SemaphoreType.DMA((SEMS,)),
        ],
        compiler_params=pltpu.CompilerParams(collective_id=0, has_side_effects=True, vmem_limit_bytes=56 << 20),
        name="advect",
    )(lat_row.T, lon_offset.T, lat_weight.T, packed, interp)
    return result.reshape(tracers.shape)


def solution(mesh):
    return jax.shard_map(
        on_device,
        mesh=mesh,
        in_specs=(
            P(None, None, "lat", "lon"),
            P("lat", None, None),
            P("lat", "lon"),
            P("lat", "lon"),
            P("lat", "lon"),
        ),
        out_specs=P(None, None, "lat", "lon"),
        check_vma=False,
    )
```

```python
import functools

import jax
import jax.numpy as jnp
from jax import lax
from jax.experimental import pallas as pl
from jax.experimental.pallas import tpu as pltpu
from jax.sharding import PartitionSpec as P

BLK = 128
LON = 16
LAT = 8
BLOCKS = 8
CH = 8
ROWS = 128
RIM = ROWS + 2
QROWS = 32
QSRC = QROWS + 2
TILE_ROWS = 8 * QSRC
POLAR_SHIFT = (-56, 25, 9, 9)
POLAR_OWN = (17, 25, 9, 9)
SLOTS = (25, 58, 26, 26)
SIDES = (("n", 2, (0, 2)), ("s", 6, (4, 6)))
PIECES = (("x", 0, 0, 6, 0), ("z", 1, 6, 2, 8))
SENDS = 51
LANDS = 51
RELAY = 16
MESH = pl.DeviceIdType.MESH


def fused_kernel(lat_row_in, lon_offset_in, lat_weight_in, tracers, interp, out,
                 fields, weight, itable, ftable, slot_of, tiles_of, south_of, north_of, tbuf, mats, t32, w0, w1, w2, w3, relay, o32, load_sem, halo_sem, send_sem, recv_sem):
    lon = lax.axis_index("lon")
    lat = lax.axis_index("lat")
    odd = (lon & 1) == 1
    far_z = (lon & 2) == 2
    polar = lat == 0
    relays = (lat == SIDES[0][1]) | (lat == SIDES[1][1])
    wins = (w0, w1, w2, w3)

    def at(lat_index, dist):
        return ((lon + dist) & (LON - 1), lat_index)

    def pick(if_odd, if_even):
        return jnp.where(odd, if_odd, if_even)

    north = (lat - 1) & (LAT - 1)
    south = (lat + 1) & (LAT - 1)
    sib = at(lat, pick(-1, 1))
    nb = at(lat, pick(1, -1))
    zdist = jnp.where(far_z, -2, 2)
    xdist = jnp.where(far_z, -4, 4)

    load_tracers = pltpu.make_async_copy(tracers, tbuf, load_sem.at[0])
    load_tracers.start()
    loads = [
        pltpu.make_async_copy(src, dst, load_sem.at[1 + i])
        for i, (src, dst) in enumerate(
            ((interp, mats), (lat_row_in, fields.at[0]), (lon_offset_in, fields.at[1]), (lat_weight_in, weight)))
    ]

    barrier = pltpu.get_barrier_semaphore()
    even = jnp.logical_not(odd)
    inner = odd != far_z
    outer = jnp.logical_not(inner)
    one = jnp.int32(1)
    none = jnp.int32(0)

    def greet(*devices):
        for d in devices:
            pl.semaphore_signal(barrier, inc=1, device_id=d, device_id_type=MESH)

    top = lat == 0
    bottom = lat == LAT - 1
    pl.when(jnp.logical_not(top))(lambda: greet((lon, north)))
    pl.when(jnp.logical_not(bottom))(lambda: greet((lon, south)))

    @pl.when(polar)
    def _():
        greet(sib, at(lat, zdist), at(lat, pick(2, -2)), at(lat, -xdist), at(lat, pick(4, -4)), at(1, pick(3, -3) + zdist),
              at(1, zdist + 8), at(lat, 8))
        pl.when(outer)(lambda: greet(nb))
        pl.when(odd)(lambda: greet(at(lat, 9)))
        for _, band, _ in SIDES:
            greet(at(band, 8), at(band, 0))
            pl.when(even)(lambda band=band: greet(at(band, jnp.where(far_z, 8, 4))))

    @pl.when(jnp.logical_not(polar))
    def _():
        greet(sib, nb)

    @pl.when(relays)
    def _():
        greet(at(0, 0), at(0, pick(1, -1)))
        pl.when(even)(lambda: greet(at(0, jnp.where(far_z, -1, 3))))

    @pl.when(lat == 1)
    def _():
        greet(at(0, zdist))

    load_tracers.wait()
    for load in loads:
        load.start()
    for g in range(BLOCKS):
        for rb in range(ROWS // 16):
            for ch in range(CH):
                part = tbuf[ch, 16 * rb : 16 * rb + 16, BLK * g : BLK * (g + 1)].astype(jnp.float32)
                t32[g, pl.ds(8 + 128 * rb + ch, 16, stride=8), :] = part

    def pack(q, low, high):
        own = jnp.where(polar, POLAR_OWN[q], 1)
        for g in range(BLOCKS):
            wins[q][own + g, low:high, :] = t32[g, 8 * QROWS * q + low : 8 * QROWS * q + high, :].astype(jnp.bfloat16)

    pack(1, 0, TILE_ROWS)
    pack(2, 0, TILE_ROWS)

    greeted = 4 - jnp.where(top | bottom, one, none) + jnp.where(polar, 9 + jnp.where(outer, one, none) + jnp.where(even, one, 2 * one), none)
    greeted = greeted + jnp.where(lat == 1, 2 * one, none) + jnp.where(relays, 2 + jnp.where(even, one, none), none)
    pl.semaphore_wait(barrier, greeted)

    down = pltpu.make_async_remote_copy(
        src_ref=t32.at[:, pl.ds(8 * ROWS, 8), :], dst_ref=t32.at[:, pl.ds(0, 8), :],
        send_sem=halo_sem.at[0], recv_sem=halo_sem.at[1], device_id=(lon, south), device_id_type=MESH)
    up = pltpu.make_async_remote_copy(
        src_ref=t32.at[:, pl.ds(8, 8), :], dst_ref=t32.at[:, pl.ds(8 * RIM - 8, 8), :],
        send_sem=halo_sem.at[2], recv_sem=halo_sem.at[3], device_id=(lon, north), device_id_type=MESH)
    pl.when(jnp.logical_not(bottom))(lambda: down.start())
    pl.when(jnp.logical_not(top))(lambda: up.start())

    started = ({}, {})
    landed = ({}, {})
    sent = []

    def number(names, name, most):
        index = names.setdefault(name, len(names))
        assert index < most, name
        return index

    def copy(name, src, dst, to):
        plain = name.startswith(("left", "right"))
        from_polar = not plain and (not name.endswith("down") or name in direct)
        to_polar = not plain and not name.endswith("up")
        return pltpu.make_async_remote_copy(
            src_ref=src, dst_ref=dst,
            send_sem=send_sem.at[number(started[from_polar], name, SENDS)],
            recv_sem=recv_sem.at[number(landed[to_polar], name, LANDS)],
            device_id=to, device_id_type=MESH)

    direct = [f"a8 {first} down" for way, _, first, _, _ in PIECES if way == "x"]

    def when(cond, body):
        if cond is None:
            body()
        else:
            pl.when(cond)(body)

    def span(ref, first, count):
        return ref, first, count

    def block_of(slots):
        ref, first, count = slots
        return ref.at[pl.ds(first, count)]

    def put(name, src, dst, to, cond=None):
        when(cond, lambda: copy(name, block_of(src), block_of(dst), to).start())
        sent.append((name, src[0], src[2], cond))

    def got(name, dst, cond=None):
        when(cond, lambda: copy(name, block_of(dst), block_of(dst), sib).wait_recv())

    def all_sent_of(entry):
        name, ref, count, cond = entry
        block = ref.at[pl.ds(0, count)]
        when(cond, lambda: copy(name, block, block, sib).wait_send())

    def all_sent():
        for entry in sent:
            all_sent_of(entry)
        sent.clear()

    compute = functools.partial(interpolate, slot_of, tiles_of, south_of, north_of, mats, out, o32)
    pairs = range(0, BLOCKS, 2)

    def tabulate():
        for load in loads:
            load.wait()

        row = lax.broadcasted_iota(jnp.int32, (BLOCKS, ROWS), 1)
        shift = jnp.where(row < QROWS, POLAR_SHIFT[0], jnp.where(row < 2 * QROWS, POLAR_SHIFT[1], POLAR_SHIFT[2]))
        shift = jnp.where(polar, shift, 1)
        back = fields[0] < lat * ROWS + row
        odd_row = (row & 1) == 1
        itable[0] = jnp.maximum(shift + fields[1] + lax.broadcasted_iota(jnp.int32, (BLOCKS, ROWS), 0), 0)
        itable[1] = jnp.where(back, 0, 8) + jnp.where(odd_row, 8, 0)
        first_south = back != odd_row
        ftable[0] = jnp.where(first_south, 1.0 - weight[...], weight[...])
        ftable[1] = jnp.where(first_south, weight[...], 1.0 - weight[...])
        tables = [
            pltpu.make_async_copy(src, dst, load_sem.at[5 + i])
            for i, (src, dst) in enumerate(
                ((itable.at[0], slot_of), (itable.at[1], tiles_of), (ftable.at[0], south_of), (ftable.at[1], north_of)))
        ]
        for table in tables:
            table.start()
        for table in tables:
            table.wait()

    def across_c(q):
        for i in range(2):
            for side, _, firsts in SIDES:
                split = q == 3
                got(f"c{q} {side}{i} down", span(wins[q], pick(17, 1) + firsts[i], 2), inner if split else None)
                if split:
                    got(f"c3 nb{firsts[i]}", span(w3, pick(17, 1) + firsts[i], 2), outer)
        put(f"c{q} one", span(wins[q], pick(17, 8), 1), span(wins[q], pick(25, 0), 1), sib)

    def finish_c(q):
        got(f"c{q} sib", span(wins[q], pick(1, 17), 8))
        got(f"c{q} end", span(wins[q], pick(25, 0), 1))
        got(f"c{q} one", span(wins[q], pick(0, 25), 1))

    def pass_x(i):
        far = jnp.where(far_z, 41, 9) + i
        got(f"b x{i}", span(w1, far, 2))
        put(f"b fx{i}", span(w1, far, 2), span(w1, jnp.where(far_z, pick(49, 33), pick(17, 1)) + i, 2), sib)

    @pl.when(polar)
    def _():
        def up_c(q, i):
            cond = inner if q == 3 else None
            for side, band, firsts in SIDES:
                put(f"c{q} {side}{i} up", span(wins[q], 9 + firsts[i], 2), span(relay, 8 + 4 * (q - 2) + 2 * i, 2),
                    at(band, pick(1, -1)), cond)

        def up_a7(i):
            for side, band, firsts in SIDES:
                put(f"a7 {side}{i} up", span(w0, 17 + firsts[i], 2), span(relay, 4 + 2 * i, 2),
                    at(band, jnp.where(far_z, -3, 1)), odd)

        def up_a8(ways):
            for way, band, first, count, slot in PIECES:
                if way not in ways:
                    continue
                if way == "x":
                    put(f"a8 {first} down", span(w0, 17 + first, count), span(w0, 8 + first, count), at(band, -8))
                else:
                    put(f"a8 {first} up", span(w0, 17 + first, count), span(relay, slot, count), at(band, zdist if way == "z" else 0))

        def left(*names):
            for name in names:
                for entry in [x for x in sent if x[0] == name]:
                    sent.remove(entry)
                    all_sent_of(entry)

        for i in pairs:
            put(f"b z{i}", span(w1, 25 + i, 2), span(w1, jnp.where(far_z, 41, 9) + i, 2), at(lat, zdist))
        up_c(2, 0)
        up_c(2, 1)
        for i in pairs:
            put(f"b far{i} up", span(w1, pick(31 - i, 25 + i), 2), span(relay, i, 2), at(1, zdist))
        put("b end", span(w1, pick(25, 32), 1), span(w1, pick(57, 0), 1), at(lat, pick(-4, 4)))
        put("b sib", span(w1, 25, 8), span(w1, pick(33, 17), 8), sib)
        put("c2 sib", span(w2, 9, 8), span(w2, pick(17, 1), 8), sib)
        put("c2 end", span(w2, pick(9, 16), 1), span(w2, pick(25, 0), 1), at(lat, pick(-2, 2)))

        for g in range(BLOCKS):
            first = t32[g, 8:16, :]
            w0[17 + g, 0:16, :] = jnp.concatenate([jnp.zeros_like(first), first], axis=0).astype(jnp.bfloat16)
        pack(0, 16, TILE_ROWS)
        up_a8(("x", "z"))
        put("a9", span(w0, 17, 1), span(w0, 16, 1), at(lat, -9), even)

        pack(3, 0, TILE_ROWS - 16)
        down.wait_send()
        up.wait_recv()
        pack(3, TILE_ROWS - 16, TILE_ROWS)
        put("c3 sib", span(w3, 9, 8), span(w3, pick(17, 1), 8), sib)
        put("c3 end", span(w3, pick(9, 16), 1), span(w3, pick(25, 0), 1), at(lat, pick(-2, 2)))

        for i in pairs:
            mine = span(w1, jnp.where(far_z, 9, 41) + i, 2)
            got(f"b z{i}", mine)
            put(f"b x{i}", mine, span(w1, jnp.where(far_z, 41, 9) + i, 2), at(lat, xdist))
            put(f"b fz{i}", mine, span(w1, jnp.where(far_z, pick(17, 1), pick(49, 33)) + i, 2), sib)
            if i == 0:
                left("c2 n0 up", "c2 s0 up")
                up_a8(("n", "s"))
                up_a7(0)
                tabulate()
            if i == 2:
                left("c2 n1 up", "c2 s1 up")
                up_c(3, 0)
            if i == 4:
                up_a7(1)
                up_c(3, 1)
                for k in pairs:
                    put(f"c3 nb{k}", span(w3, 9 + k, 2), span(w3, pick(1, 17) + k, 2), nb, outer)
            if i >= 4:
                pass_x(i - 4)
            if i == 4:
                across_c(2)
        finish_c(2)

    polar_sent = list(sent)
    sent.clear()

    @pl.when(jnp.logical_not(polar))
    def _():
        def sides(q):
            put(f"left {q}", span(wins[q], 1, 1), span(wins[q], 9, 1), at(lat, -1))
            put(f"right {q}", span(wins[q], 8, 1), span(wins[q], 0, 1), at(lat, 1))

        passed = []

        def on_the_way(stage):
            plain = list(sent)

            def pass_on(name, slot, count, win, first, dist, cond=None):
                block = span(relay, slot, count)
                got(f"{name} up", block, cond)
                put(f"{name} down", block, span(win, first, count), at(0, dist), cond)

            @pl.when(lat == 1)
            def _():
                sent.clear()
                if stage == 0:
                    pass_on("b far0", 0, 2, w1, pick(7, 49), zdist + pick(3, -3))
                else:
                    for i in pairs[1:]:
                        pass_on(f"b far{i}", i, 2, w1, pick(7 - i, 49 + i), zdist + pick(3, -3))
                    for way, _, first, count, slot in PIECES:
                        if way == "z":
                            pass_on(f"a8 {first}", slot, count, w0, 8 + first, zdist - 8)
                passed.extend((1, x) for x in sent)

            for side, band, firsts in SIDES:
                @pl.when(lat == band)
                def _(side=side, band=band, firsts=firsts):
                    sent.clear()
                    if stage == 0:
                        for i in range(2):
                            pass_on(f"c2 {side}{i}", 8 + 2 * i, 2, w2, pick(17, 1) + firsts[i], 0)
                    else:
                        for way, _, first, count, slot in PIECES:
                            if way == side:
                                pass_on(f"a8 {first}", slot, count, w0, 8 + first, -8)
                        for i in range(2):
                            pass_on(f"a7 {side}{i}", 4 + 2 * i, 2, w0, firsts[i], jnp.where(far_z, -8, -4), even)
                            pass_on(f"c3 {side}{i}", 12 + 2 * i, 2, w3, pick(17, 1) + firsts[i], 0, inner)
                    passed.extend((band, x) for x in sent)

            sent.clear()
            sent.extend(plain)

        sides(1)
        sides(2)
        on_the_way(0)
        pack(0, 16, TILE_ROWS)
        pack(3, 0, TILE_ROWS - 16)
        up.wait_send()
        down.wait_recv()

        @pl.when(jnp.logical_not(bottom))
        def _():
            down.wait_send()
            up.wait_recv()

        @pl.when(bottom)
        def _():
            t32[:, 8 * RIM - 8 : 8 * RIM, :] = jnp.zeros((BLOCKS, 8, BLK), jnp.float32)

        pack(0, 0, 16)
        pack(3, TILE_ROWS - 16, TILE_ROWS)
        sides(0)
        sides(3)
        tabulate()
        on_the_way(1)
        plain = list(sent)
        for band in (1, 2, 6):
            @pl.when(lat == band)
            def _(band=band):
                sent.clear()
                sent.extend(x for at_band, x in passed if at_band == band)
                all_sent()

        sent.clear()
        sent.extend(plain)

        for q in range(4):
            got(f"left {q}", span(wins[q], 9, 1))
            got(f"right {q}", span(wins[q], 0, 1))

    plain_sent = list(sent)
    sent.clear()
    sent.extend(polar_sent)

    compute(2, w2)

    @pl.when(polar)
    def _():
        early = list(sent)
        pass_x(4)
        got("b far0 down", span(w1, pick(49, 7), 2))
        put("b one", span(w1, pick(49, 8), 1), span(w1, pick(57, 0), 1), sib)
        for _, _, first, count, _ in PIECES:
            got(f"a8 {first} down", span(w0, 8 + first, count))
            put(f"a f {first}", span(w0, 8 + first, count), span(w0, first, count), sib, even)
            if first == 0:
                put("a one", span(w0, 8, 1), span(w0, 16, 1), sib, odd)
        for entry in early:
            if not entry[0].startswith(("c3 nb", "b x6", "b fz6", "c3 n1", "c3 s1")):
                sent.remove(entry)
                all_sent_of(entry)
        pass_x(6)
        across_c(3)
        for i in range(2):
            for side, _, firsts in SIDES:
                got(f"a7 {side}{i} down", span(w0, firsts[i], 2), even)
        for _, _, first, count, _ in PIECES:
            got(f"a f {first}", span(w0, first, count), odd)
        got("a9", span(w0, 16, 1), odd)
        got("a one", span(w0, 16, 1), even)

    compute(0, w0)

    @pl.when(polar)
    def _():
        finish_c(3)

    compute(3, w3)

    @pl.when(polar)
    def _():
        for i in pairs[1:]:
            got(f"b far{i} down", span(w1, pick(49 + i, 7 - i), 2))
        got("b end", span(w1, pick(57, 0), 1))
        got("b sib", span(w1, pick(17, 33), 8))
        for i in pairs:
            got(f"b fz{i}", span(w1, jnp.where(far_z, pick(1, 17), pick(33, 49)) + i, 2))
            got(f"b fx{i}", span(w1, jnp.where(far_z, pick(33, 49), pick(1, 17)) + i, 2))
        got("b one", span(w1, pick(0, 57), 1))

    compute(1, w1)

    @pl.when(polar)
    def _():
        all_sent()

    sent.extend(plain_sent)

    @pl.when(jnp.logical_not(polar))
    def _():
        all_sent()


def interpolate(slot_of, tiles_of, south_of, north_of, mats, out, o32, q, window):
    sublane = lax.broadcasted_iota(jnp.int32, (16, BLK), 0)

    for part in range(2):
        for j in range(16):
            start = 128 * part + 16 * (j // 2)
            row = QROWS * q + 16 * part + j
            lead, trail = [], []
            for b in range(BLOCKS):
                g = slot_of[b, row]
                lower = sublane < tiles_of[b, row]
                for tiles, slot in ((lead, g), (trail, g + 1)):
                    tiles.append(jnp.where(lower, window[slot, pl.ds(start + 16, 16), :], window[slot, pl.ds(start, 16), :]))
            lhs = jnp.concatenate([jnp.concatenate(lead, axis=0), jnp.concatenate(trail, axis=0)], axis=1)
            prod = jnp.dot(lhs, mats[row], preferred_element_type=jnp.float32)
            for b in range(BLOCKS):
                at = 16 * b
                o32[b, 8 * j : 8 * j + 8, :] = south_of[b, row] * prod[at : at + 8] + north_of[b, row] * prod[at + 8 : at + 16]
        low = QROWS * q + 16 * part
        for b in range(BLOCKS):
            for ch in range(CH):
                out[ch, low : low + 16, BLK * b : BLK * (b + 1)] = o32[b, pl.ds(ch, 16, stride=8), :].astype(jnp.bfloat16)


def on_device(tracers, interp, lat_weight, lat_row, lon_offset):
    packed = tracers.reshape(CH, ROWS, BLOCKS * BLK)
    anywhere = pl.BlockSpec(memory_space=pl.ANY)
    result = pl.pallas_call(
        fused_kernel,
        out_shape=pltpu.VMEM((CH, ROWS, BLOCKS * BLK), jnp.bfloat16),
        in_specs=[anywhere] * 5,
        out_specs=pl.BlockSpec(memory_space=pltpu.VMEM),
        scratch_shapes=[
            pltpu.VMEM((2, BLOCKS, ROWS), jnp.int32),
            pltpu.VMEM((BLOCKS, ROWS), jnp.float32),
            pltpu.VMEM((2, BLOCKS, ROWS), jnp.int32),
            pltpu.VMEM((2, BLOCKS, ROWS), jnp.float32),
            pltpu.SMEM((BLOCKS, ROWS), jnp.int32),
            pltpu.SMEM((BLOCKS, ROWS), jnp.int32),
            pltpu.SMEM((BLOCKS, ROWS), jnp.float32),
            pltpu.SMEM((BLOCKS, ROWS), jnp.float32),
            pltpu.VMEM((CH, ROWS, BLOCKS * BLK), jnp.bfloat16),
            pltpu.VMEM((ROWS, 2 * BLK, BLK), jnp.bfloat16),
            pltpu.VMEM((BLOCKS, 8 * RIM, BLK), jnp.float32),
        ] + [pltpu.VMEM((n, TILE_ROWS, BLK), jnp.bfloat16) for n in SLOTS] + [
            pltpu.VMEM((RELAY, TILE_ROWS, BLK), jnp.bfloat16),
            pltpu.VMEM((BLOCKS, 8 * 16, BLK), jnp.float32),
            pltpu.SemaphoreType.DMA((9,)),
            pltpu.SemaphoreType.DMA((4,)),
            pltpu.SemaphoreType.DMA((SENDS,)),
            pltpu.SemaphoreType.DMA((LANDS,)),
        ],
        compiler_params=pltpu.CompilerParams(collective_id=0, has_side_effects=True, vmem_limit_bytes=56 << 20),
        name="advect",
    )(lat_row.T, lon_offset.T, lat_weight.T, packed, interp)
    return result.reshape(tracers.shape)


def solution(mesh):
    return jax.shard_map(
        on_device,
        mesh=mesh,
        in_specs=(
            P(None, None, "lat", "lon"),
            P("lat", None, None),
            P("lat", "lon"),
            P("lat", "lon"),
            P("lat", "lon"),
        ),
        out_specs=P(None, None, "lat", "lon"),
        check_vma=False,
    )
```

```python
import functools

import jax
import jax.numpy as jnp
from jax import lax
from jax.experimental import pallas as pl
from jax.experimental.pallas import tpu as pltpu
from jax.sharding import PartitionSpec as P

BLK = 128
LON = 16
LAT = 8
BLOCKS = 8
CH = 8
ROWS = 128
RIM = ROWS + 2
QROWS = 32
QSRC = QROWS + 2
TILE_ROWS = 8 * QSRC
POLAR_SHIFT = (-56, 25, 9, 9)
POLAR_OWN = (17, 25, 9, 9)
SLOTS = (25, 58, 26, 26)
SIDES = (("n", 2, (0, 2)), ("s", 6, (4, 6)))
PIECES = (("x", 0, 0, 6, 0), ("z", 1, 6, 2, 8))
SENDS = 51
LANDS = 51
RELAY = 16
MESH = pl.DeviceIdType.MESH


def fused_kernel(lat_row_in, lon_offset_in, lat_weight_in, tracers, interp, out,
                 fields, weight, itable, ftable, slot_of, tiles_of, south_of, north_of, tbuf, mats, t32, w0, w1, w2, w3, relay, o32, load_sem, halo_sem, send_sem, recv_sem):
    lon = lax.axis_index("lon")
    lat = lax.axis_index("lat")
    odd = (lon & 1) == 1
    far_z = (lon & 2) == 2
    polar = lat == 0
    relays = (lat == SIDES[0][1]) | (lat == SIDES[1][1])
    wins = (w0, w1, w2, w3)

    def at(lat_index, dist):
        return ((lon + dist) & (LON - 1), lat_index)

    def pick(if_odd, if_even):
        return jnp.where(odd, if_odd, if_even)

    north = (lat - 1) & (LAT - 1)
    south = (lat + 1) & (LAT - 1)
    sib = at(lat, pick(-1, 1))
    nb = at(lat, pick(1, -1))
    zdist = jnp.where(far_z, -2, 2)
    xdist = jnp.where(far_z, -4, 4)

    load_tracers = pltpu.make_async_copy(tracers, tbuf, load_sem.at[0])
    load_tracers.start()
    loads = [
        pltpu.make_async_copy(src, dst, load_sem.at[1 + i])
        for i, (src, dst) in enumerate(
            ((interp, mats), (lat_row_in, fields.at[0]), (lon_offset_in, fields.at[1]), (lat_weight_in, weight)))
    ]

    barrier = pltpu.get_barrier_semaphore()
    even = jnp.logical_not(odd)
    inner = odd != far_z
    outer = jnp.logical_not(inner)
    one = jnp.int32(1)
    none = jnp.int32(0)

    def greet(*devices):
        for d in devices:
            pl.semaphore_signal(barrier, inc=1, device_id=d, device_id_type=MESH)

    top = lat == 0
    bottom = lat == LAT - 1
    pl.when(jnp.logical_not(top))(lambda: greet((lon, north)))
    pl.when(jnp.logical_not(bottom))(lambda: greet((lon, south)))

    @pl.when(polar)
    def _():
        greet(sib, at(lat, zdist), at(lat, pick(2, -2)), at(lat, -xdist), at(lat, pick(4, -4)), at(1, pick(3, -3) + zdist),
              at(1, zdist + 8), at(lat, 8))
        pl.when(outer)(lambda: greet(nb))
        pl.when(odd)(lambda: greet(at(lat, 9)))
        for _, band, _ in SIDES:
            greet(at(band, 8), at(band, 0))
            pl.when(even)(lambda band=band: greet(at(band, jnp.where(far_z, 8, 4))))

    @pl.when(jnp.logical_not(polar))
    def _():
        greet(sib, nb)

    @pl.when(relays)
    def _():
        greet(at(0, 0), at(0, pick(1, -1)))
        pl.when(even)(lambda: greet(at(0, jnp.where(far_z, -1, 3))))

    @pl.when(lat == 1)
    def _():
        greet(at(0, zdist))

    load_tracers.wait()
    for load in loads:
        load.start()
    for g in range(BLOCKS):
        for rb in range(ROWS // 16):
            for ch in range(CH):
                part = tbuf[ch, 16 * rb : 16 * rb + 16, BLK * g : BLK * (g + 1)].astype(jnp.float32)
                t32[g, pl.ds(8 + 128 * rb + ch, 16, stride=8), :] = part

    def pack(q, low, high):
        own = jnp.where(polar, POLAR_OWN[q], 1)
        for g in range(BLOCKS):
            wins[q][own + g, low:high, :] = t32[g, 8 * QROWS * q + low : 8 * QROWS * q + high, :].astype(jnp.bfloat16)

    pack(1, 0, TILE_ROWS)
    pack(2, 0, TILE_ROWS)

    greeted = 4 - jnp.where(top | bottom, one, none) + jnp.where(polar, 9 + jnp.where(outer, one, none) + jnp.where(even, one, 2 * one), none)
    greeted = greeted + jnp.where(lat == 1, 2 * one, none) + jnp.where(relays, 2 + jnp.where(even, one, none), none)
    pl.semaphore_wait(barrier, greeted)

    down = pltpu.make_async_remote_copy(
        src_ref=t32.at[:, pl.ds(8 * ROWS, 8), :], dst_ref=t32.at[:, pl.ds(0, 8), :],
        send_sem=halo_sem.at[0], recv_sem=halo_sem.at[1], device_id=(lon, south), device_id_type=MESH)
    up = pltpu.make_async_remote_copy(
        src_ref=t32.at[:, pl.ds(8, 8), :], dst_ref=t32.at[:, pl.ds(8 * RIM - 8, 8), :],
        send_sem=halo_sem.at[2], recv_sem=halo_sem.at[3], device_id=(lon, north), device_id_type=MESH)
    pl.when(jnp.logical_not(bottom))(lambda: down.start())
    pl.when(jnp.logical_not(top))(lambda: up.start())

    started = ({}, {})
    landed = ({}, {})
    sent = []

    def number(names, name, most):
        index = names.setdefault(name, len(names))
        assert index < most, name
        return index

    def copy(name, src, dst, to):
        plain = name.startswith(("left", "right"))
        from_polar = not plain and (not name.endswith("down") or name in direct)
        to_polar = not plain and not name.endswith("up")
        return pltpu.make_async_remote_copy(
            src_ref=src, dst_ref=dst,
            send_sem=send_sem.at[number(started[from_polar], name, SENDS)],
            recv_sem=recv_sem.at[number(landed[to_polar], name, LANDS)],
            device_id=to, device_id_type=MESH)

    direct = [f"a8 {first} down" for way, _, first, _, _ in PIECES if way == "x"]

    def when(cond, body):
        if cond is None:
            body()
        else:
            pl.when(cond)(body)

    def span(ref, first, count):
        return ref, first, count

    def block_of(slots):
        ref, first, count = slots
        return ref.at[pl.ds(first, count)]

    def put(name, src, dst, to, cond=None):
        when(cond, lambda: copy(name, block_of(src), block_of(dst), to).start())
        sent.append((name, src[0], src[2], cond))

    def got(name, dst, cond=None):
        when(cond, lambda: copy(name, block_of(dst), block_of(dst), sib).wait_recv())

    def all_sent_of(entry):
        name, ref, count, cond = entry
        block = ref.at[pl.ds(0, count)]
        when(cond, lambda: copy(name, block, block, sib).wait_send())

    def all_sent():
        for entry in sent:
            all_sent_of(entry)
        sent.clear()

    compute = functools.partial(interpolate, slot_of, tiles_of, south_of, north_of, mats, out, o32)
    pairs = range(0, BLOCKS, 2)

    def tabulate():
        for load in loads:
            load.wait()

        row = lax.broadcasted_iota(jnp.int32, (BLOCKS, ROWS), 1)
        shift = jnp.where(row < QROWS, POLAR_SHIFT[0], jnp.where(row < 2 * QROWS, POLAR_SHIFT[1], POLAR_SHIFT[2]))
        shift = jnp.where(polar, shift, 1)
        back = fields[0] < lat * ROWS + row
        odd_row = (row & 1) == 1
        itable[0] = jnp.maximum(shift + fields[1] + lax.broadcasted_iota(jnp.int32, (BLOCKS, ROWS), 0), 0)
        itable[1] = jnp.where(back, 0, 8) + jnp.where(odd_row, 8, 0)
        first_south = back != odd_row
        ftable[0] = jnp.where(first_south, 1.0 - weight[...], weight[...])
        ftable[1] = jnp.where(first_south, weight[...], 1.0 - weight[...])
        tables = [
            pltpu.make_async_copy(src, dst, load_sem.at[5 + i])
            for i, (src, dst) in enumerate(
                ((itable.at[0], slot_of), (itable.at[1], tiles_of), (ftable.at[0], south_of), (ftable.at[1], north_of)))
        ]
        for table in tables:
            table.start()
        for table in tables:
            table.wait()

    def across_c(q):
        for i in range(2):
            for side, _, firsts in SIDES:
                split = q == 3
                got(f"c{q} {side}{i} down", span(wins[q], pick(17, 1) + firsts[i], 2), inner if split else None)
                if split:
                    got(f"c3 nb{firsts[i]}", span(w3, pick(17, 1) + firsts[i], 2), outer)
        put(f"c{q} one", span(wins[q], pick(17, 8), 1), span(wins[q], pick(25, 0), 1), sib)

    def finish_c(q):
        got(f"c{q} sib", span(wins[q], pick(1, 17), 8))
        got(f"c{q} end", span(wins[q], pick(25, 0), 1))
        got(f"c{q} one", span(wins[q], pick(0, 25), 1))

    def pass_x(i):
        far = jnp.where(far_z, 41, 9) + i
        got(f"b x{i}", span(w1, far, 2))
        put(f"b fx{i}", span(w1, far, 2), span(w1, jnp.where(far_z, pick(49, 33), pick(17, 1)) + i, 2), sib)

    @pl.when(polar)
    def _():
        def up_c(q, i):
            cond = inner if q == 3 else None
            for side, band, firsts in SIDES:
                put(f"c{q} {side}{i} up", span(wins[q], 9 + firsts[i], 2), span(relay, 8 + 4 * (q - 2) + 2 * i, 2),
                    at(band, pick(1, -1)), cond)

        def up_a7(i):
            for side, band, firsts in SIDES:
                put(f"a7 {side}{i} up", span(w0, 17 + firsts[i], 2), span(relay, 4 + 2 * i, 2),
                    at(band, jnp.where(far_z, -3, 1)), odd)

        def up_a8(ways):
            for way, band, first, count, slot in PIECES:
                if way not in ways:
                    continue
                if way == "x":
                    put(f"a8 {first} down", span(w0, 17 + first, count), span(w0, 8 + first, count), at(band, -8))
                else:
                    put(f"a8 {first} up", span(w0, 17 + first, count), span(relay, slot, count), at(band, zdist if way == "z" else 0))

        def left(*names):
            for name in names:
                for entry in [x for x in sent if x[0] == name]:
                    sent.remove(entry)
                    all_sent_of(entry)

        for i in pairs:
            put(f"b z{i}", span(w1, 25 + i, 2), span(w1, jnp.where(far_z, 41, 9) + i, 2), at(lat, zdist))
        up_c(2, 0)
        up_c(2, 1)
        def up_far(*firsts):
            for i in firsts:
                put(f"b far{i} up", span(w1, pick(31 - i, 25 + i), 2), span(relay, i, 2), at(1, zdist))

        up_far(0, 2)
        put("b end", span(w1, pick(25, 32), 1), span(w1, pick(57, 0), 1), at(lat, pick(-4, 4)))
        put("b sib", span(w1, 25, 8), span(w1, pick(33, 17), 8), sib)
        put("c2 sib", span(w2, 9, 8), span(w2, pick(17, 1), 8), sib)
        put("c2 end", span(w2, pick(9, 16), 1), span(w2, pick(25, 0), 1), at(lat, pick(-2, 2)))

        for g in range(BLOCKS):
            first = t32[g, 8:16, :]
            w0[17 + g, 0:16, :] = jnp.concatenate([jnp.zeros_like(first), first], axis=0).astype(jnp.bfloat16)
        pack(0, 16, TILE_ROWS)
        up_a8(("x", "z"))
        up_far(4, 6)
        put("a9", span(w0, 17, 1), span(w0, 16, 1), at(lat, -9), even)

        pack(3, 0, TILE_ROWS - 16)
        down.wait_send()
        up.wait_recv()
        pack(3, TILE_ROWS - 16, TILE_ROWS)
        put("c3 sib", span(w3, 9, 8), span(w3, pick(17, 1), 8), sib)
        put("c3 end", span(w3, pick(9, 16), 1), span(w3, pick(25, 0), 1), at(lat, pick(-2, 2)))

        for i in pairs:
            mine = span(w1, jnp.where(far_z, 9, 41) + i, 2)
            got(f"b z{i}", mine)
            put(f"b x{i}", mine, span(w1, jnp.where(far_z, 41, 9) + i, 2), at(lat, xdist))
            put(f"b fz{i}", mine, span(w1, jnp.where(far_z, pick(17, 1), pick(49, 33)) + i, 2), sib)
            if i == 0:
                left("c2 n0 up", "c2 s0 up")
                up_a8(("n", "s"))
                up_a7(0)
                tabulate()
            if i == 2:
                left("c2 n1 up", "c2 s1 up")
                up_c(3, 0)
            if i == 4:
                up_a7(1)
                up_c(3, 1)
                for k in pairs:
                    put(f"c3 nb{k}", span(w3, 9 + k, 2), span(w3, pick(1, 17) + k, 2), nb, outer)
            if i >= 4:
                pass_x(i - 4)
            if i == 4:
                across_c(2)
        finish_c(2)

    polar_sent = list(sent)
    sent.clear()

    @pl.when(jnp.logical_not(polar))
    def _():
        def sides(q):
            put(f"left {q}", span(wins[q], 1, 1), span(wins[q], 9, 1), at(lat, -1))
            put(f"right {q}", span(wins[q], 8, 1), span(wins[q], 0, 1), at(lat, 1))

        passed = []

        def on_the_way(stage):
            plain = list(sent)

            def pass_on(name, slot, count, win, first, dist, cond=None):
                block = span(relay, slot, count)
                got(f"{name} up", block, cond)
                put(f"{name} down", block, span(win, first, count), at(0, dist), cond)

            @pl.when(lat == 1)
            def _():
                sent.clear()
                if stage == 0:
                    pass_on("b far0", 0, 2, w1, pick(7, 49), zdist + pick(3, -3))
                else:
                    for i in pairs[1:]:
                        pass_on(f"b far{i}", i, 2, w1, pick(7 - i, 49 + i), zdist + pick(3, -3))
                        for way, _, first, count, slot in PIECES:
                            if way == "z" and i == 2:
                                pass_on(f"a8 {first}", slot, count, w0, 8 + first, zdist - 8)
                passed.extend((1, x) for x in sent)

            for side, band, firsts in SIDES:
                @pl.when(lat == band)
                def _(side=side, band=band, firsts=firsts):
                    sent.clear()
                    if stage == 0:
                        for i in range(2):
                            pass_on(f"c2 {side}{i}", 8 + 2 * i, 2, w2, pick(17, 1) + firsts[i], 0)
                    else:
                        for way, _, first, count, slot in PIECES:
                            if way == side:
                                pass_on(f"a8 {first}", slot, count, w0, 8 + first, -8)
                        for i in range(2):
                            pass_on(f"a7 {side}{i}", 4 + 2 * i, 2, w0, firsts[i], jnp.where(far_z, -8, -4), even)
                            pass_on(f"c3 {side}{i}", 12 + 2 * i, 2, w3, pick(17, 1) + firsts[i], 0, inner)
                    passed.extend((band, x) for x in sent)

            sent.clear()
            sent.extend(plain)

        sides(1)
        sides(2)
        on_the_way(0)
        pack(0, 16, TILE_ROWS)
        pack(3, 0, TILE_ROWS - 16)
        up.wait_send()
        down.wait_recv()

        @pl.when(jnp.logical_not(bottom))
        def _():
            down.wait_send()
            up.wait_recv()

        @pl.when(bottom)
        def _():
            t32[:, 8 * RIM - 8 : 8 * RIM, :] = jnp.zeros((BLOCKS, 8, BLK), jnp.float32)

        pack(0, 0, 16)
        pack(3, TILE_ROWS - 16, TILE_ROWS)
        sides(0)
        sides(3)
        tabulate()
        on_the_way(1)
        plain = list(sent)
        for band in (1, 2, 6):
            @pl.when(lat == band)
            def _(band=band):
                sent.clear()
                sent.extend(x for at_band, x in passed if at_band == band)
                all_sent()

        sent.clear()
        sent.extend(plain)

        for q in range(4):
            got(f"left {q}", span(wins[q], 9, 1))
            got(f"right {q}", span(wins[q], 0, 1))

    plain_sent = list(sent)
    sent.clear()
    sent.extend(polar_sent)

    compute(2, w2)

    @pl.when(polar)
    def _():
        early = list(sent)
        pass_x(4)
        got("b far0 down", span(w1, pick(49, 7), 2))
        put("b one", span(w1, pick(49, 8), 1), span(w1, pick(57, 0), 1), sib)
        for _, _, first, count, _ in PIECES:
            got(f"a8 {first} down", span(w0, 8 + first, count))
            put(f"a f {first}", span(w0, 8 + first, count), span(w0, first, count), sib, even)
            if first == 0:
                put("a one", span(w0, 8, 1), span(w0, 16, 1), sib, odd)
        for entry in early:
            if not entry[0].startswith(("c3 nb", "b x6", "b fz6", "c3 n1", "c3 s1")):
                sent.remove(entry)
                all_sent_of(entry)
        pass_x(6)
        across_c(3)
        for i in range(2):
            for side, _, firsts in SIDES:
                got(f"a7 {side}{i} down", span(w0, firsts[i], 2), even)
        for _, _, first, count, _ in PIECES:
            got(f"a f {first}", span(w0, first, count), odd)
        got("a9", span(w0, 16, 1), odd)
        got("a one", span(w0, 16, 1), even)

    compute(0, w0)

    @pl.when(polar)
    def _():
        finish_c(3)

    compute(3, w3)

    @pl.when(polar)
    def _():
        for i in pairs[1:]:
            got(f"b far{i} down", span(w1, pick(49 + i, 7 - i), 2))
        got("b end", span(w1, pick(57, 0), 1))
        got("b sib", span(w1, pick(17, 33), 8))
        for i in pairs:
            got(f"b fz{i}", span(w1, jnp.where(far_z, pick(1, 17), pick(33, 49)) + i, 2))
            got(f"b fx{i}", span(w1, jnp.where(far_z, pick(33, 49), pick(1, 17)) + i, 2))
        got("b one", span(w1, pick(0, 57), 1))

    compute(1, w1)

    @pl.when(polar)
    def _():
        all_sent()

    sent.extend(plain_sent)

    @pl.when(jnp.logical_not(polar))
    def _():
        all_sent()


def interpolate(slot_of, tiles_of, south_of, north_of, mats, out, o32, q, window):
    sublane = lax.broadcasted_iota(jnp.int32, (16, BLK), 0)

    for part in range(2):
        for j in range(16):
            start = 128 * part + 16 * (j // 2)
            row = QROWS * q + 16 * part + j
            lead, trail = [], []
            for b in range(BLOCKS):
                g = slot_of[b, row]
                lower = sublane < tiles_of[b, row]
                for tiles, slot in ((lead, g), (trail, g + 1)):
                    tiles.append(jnp.where(lower, window[slot, pl.ds(start + 16, 16), :], window[slot, pl.ds(start, 16), :]))
            lhs = jnp.concatenate([jnp.concatenate(lead, axis=0), jnp.concatenate(trail, axis=0)], axis=1)
            prod = jnp.dot(lhs, mats[row], preferred_element_type=jnp.float32)
            for b in range(BLOCKS):
                at = 16 * b
                o32[b, 8 * j : 8 * j + 8, :] = south_of[b, row] * prod[at : at + 8] + north_of[b, row] * prod[at + 8 : at + 16]
        low = QROWS * q + 16 * part
        for b in range(BLOCKS):
            for ch in range(CH):
                out[ch, low : low + 16, BLK * b : BLK * (b + 1)] = o32[b, pl.ds(ch, 16, stride=8), :].astype(jnp.bfloat16)


def on_device(tracers, interp, lat_weight, lat_row, lon_offset):
    packed = tracers.reshape(CH, ROWS, BLOCKS * BLK)
    anywhere = pl.BlockSpec(memory_space=pl.ANY)
    result = pl.pallas_call(
        fused_kernel,
        out_shape=pltpu.VMEM((CH, ROWS, BLOCKS * BLK), jnp.bfloat16),
        in_specs=[anywhere] * 5,
        out_specs=pl.BlockSpec(memory_space=pltpu.VMEM),
        scratch_shapes=[
            pltpu.VMEM((2, BLOCKS, ROWS), jnp.int32),
            pltpu.VMEM((BLOCKS, ROWS), jnp.float32),
            pltpu.VMEM((2, BLOCKS, ROWS), jnp.int32),
            pltpu.VMEM((2, BLOCKS, ROWS), jnp.float32),
            pltpu.SMEM((BLOCKS, ROWS), jnp.int32),
            pltpu.SMEM((BLOCKS, ROWS), jnp.int32),
            pltpu.SMEM((BLOCKS, ROWS), jnp.float32),
            pltpu.SMEM((BLOCKS, ROWS), jnp.float32),
            pltpu.VMEM((CH, ROWS, BLOCKS * BLK), jnp.bfloat16),
            pltpu.VMEM((ROWS, 2 * BLK, BLK), jnp.bfloat16),
            pltpu.VMEM((BLOCKS, 8 * RIM, BLK), jnp.float32),
        ] + [pltpu.VMEM((n, TILE_ROWS, BLK), jnp.bfloat16) for n in SLOTS] + [
            pltpu.VMEM((RELAY, TILE_ROWS, BLK), jnp.bfloat16),
            pltpu.VMEM((BLOCKS, 8 * 16, BLK), jnp.float32),
            pltpu.SemaphoreType.DMA((9,)),
            pltpu.SemaphoreType.DMA((4,)),
            pltpu.SemaphoreType.DMA((SENDS,)),
            pltpu.SemaphoreType.DMA((LANDS,)),
        ],
        compiler_params=pltpu.CompilerParams(collective_id=0, has_side_effects=True, vmem_limit_bytes=56 << 20),
        name="advect",
    )(lat_row.T, lon_offset.T, lat_weight.T, packed, interp)
    return result.reshape(tracers.shape)


def solution(mesh):
    return jax.shard_map(
        on_device,
        mesh=mesh,
        in_specs=(
            P(None, None, "lat", "lon"),
            P("lat", None, None),
            P("lat", "lon"),
            P("lat", "lon"),
            P("lat", "lon"),
        ),
        out_specs=P(None, None, "lat", "lon"),
        check_vma=False,
    )
```
